768 devices in a mesh: feat: 96 (over z, y), batch: 8 (over x, core).
Axes of the slice: x: 4, y: 8, z: 12, core: 2. Of those that a mesh axis runs over, the one named last changes fastest.
Arguments:
- features: bfloat16 [1056, 65536], P('feat'), may hold values from -6 to 6
- nbr_ids: int32 [16896, 15], P('batch'), may hold values from 0 to 65535
- nbr_counts: int32 [16896], P('batch'), may hold values from 1 to 15
- self_ids: int32 [16896], P('batch'), may hold values from 0 to 65535
- seed_counts: int32 [1536], P('batch'), may hold values from 1 to 10
- labels: int32 [1536], P('batch'), may hold values from 0 to 171
- w1_self: bfloat16 [1056, 256], P('feat'), may hold values from -0.1875 to 0.1875
- w1_nbr: bfloat16 [1056, 256], P('feat'), may hold values from -0.1875 to 0.1875
- w2_self: bfloat16 [256, 256], replicated, may hold values from -0.375 to 0.375
- w2_nbr: bfloat16 [256, 256], replicated, may hold values from -0.375 to 0.375
- w3: bfloat16 [256, 172], replicated, may hold values from -0.375 to 0.375
Outputs:
- dw1_self: float32 [1056, 256], P('feat')
- dw1_nbr: float32 [1056, 256], P('feat')
- dw2_self: float32 [256, 256], replicated
- dw2_nbr: float32 [256, 256], replicated
- dw3: float32 [256, 172], replicated
The draws below stay inside these ranges and needn't reach their ends.
Inputs may be any that keep to these rules, and one draw needn't show every extreme that they name: `nbr_ids`: ids beyond a target's count are padding and unused.
All inputs are finite; a program needn't handle non-finite values.
Results may differ from the reference program's by a relative error of at most 0.0059.
Values may be sent and summed in bfloat16 or wider, within the bound.
No kernel may reach another device: no remote copies, remote signals or barrier semaphores. Data moves between devices by JAX's collectives and lax.ppermute only.
A program may use at most 64 MiB of HBM per device.

```python
import jax
import jax.numpy as jnp
from jax import lax

F = 1056
H = 256
C = 172
FAN1 = 15
FAN2 = 10
NODES = 65536
ROWS_B = 2112
SEEDS = 1536
ROWS = 16896
N_BATCH = 8


def place_ends(result, rng, low, largest):
    longest = result.shape.index(max(result.shape))
    spots = []
    for shift in (0, 1):
        where = [jax.random.randint(jax.random.fold_in(rng, axis), (), 0, length) for axis, length in enumerate(result.shape)]
        where[longest] = (where[longest] + shift) % result.shape[longest]
        spots.append(tuple(where))
    return result.at[spots[0]].set(low).at[spots[1]].set(largest)


def block_scale(own_key, dims, shards, smallest, high):
    loudness = 1.0
    for axis_at, shards_of in shards:
        steps = jax.random.uniform(jax.random.fold_in(jax.random.fold_in(own_key, 6), axis_at), (shards_of,), jnp.float32, smallest / len(shards), high / len(shards))
        loudness = loudness * jnp.repeat(jnp.exp(steps), dims[axis_at] // shards_of).reshape((-1,) + (1,) * (len(dims) - 1 - axis_at))
    return loudness


def centred(key, shape, scale, reach, pieces=(), held_as=jnp.bfloat16):
    level = block_scale(key, shape, pieces, -0.22, 0.18) if pieces else 1.0
    values = jax.random.normal(key, shape, jnp.float32) * scale * level
    return jnp.minimum(jnp.maximum(values, -reach), reach).astype(held_as)


def setup_inputs(seed: int = 0) -> dict:
    splits = jax.random.split(jax.random.key(seed), 12)
    features = centred(splits[0], (F, NODES), 1.0, 6.0, ((0, 96),))
    nbr_ids = place_ends(jax.random.randint(splits[1], (ROWS, FAN1), 0, NODES), jax.random.fold_in(splits[1], 1), 0, NODES - 1).astype(jnp.int32)
    nbr_counts = place_ends(jax.random.randint(splits[2], (ROWS,), 1, FAN1 + 1), jax.random.fold_in(splits[2], 1), 1, FAN1).astype(jnp.int32)
    self_ids = place_ends(jax.random.randint(splits[3], (ROWS,), 0, NODES), jax.random.fold_in(splits[3], 1), 0, NODES - 1).astype(jnp.int32)
    seed_counts = place_ends(jax.random.randint(splits[4], (SEEDS,), 1, FAN2 + 1), jax.random.fold_in(splits[4], 1), 1, FAN2).astype(jnp.int32)
    labels = place_ends(jax.random.randint(splits[5], (SEEDS,), 0, C), jax.random.fold_in(splits[5], 1), 0, C - 1).astype(jnp.int32)
    w1_self = centred(splits[6], (F, H), F ** -0.5, 0.1875, ((0, 96),))
    w1_nbr = centred(splits[7], (F, H), F ** -0.5, 0.1875, ((0, 96),))
    w2_self = centred(splits[8], (H, H), H ** -0.5, 0.375)
    w2_nbr = centred(splits[9], (H, H), H ** -0.5, 0.375)
    w3 = centred(splits[10], (H, C), H ** -0.5, 0.375)
    return {"features": features, "nbr_ids": nbr_ids, "nbr_counts": nbr_counts, "self_ids": self_ids, "seed_counts": seed_counts, "labels": labels, "w1_self": w1_self, "w1_nbr": w1_nbr, "w2_self": w2_self, "w2_nbr": w2_nbr, "w3": w3}


def inner_rows(left, right):
    return lax.dot_general(left, right, (((0,), (0,)), ((), ())), preferred_element_type=jnp.float32)


def outer_cols(left, right):
    return lax.dot_general(left, right, (((1,), (1,)), ((), ())), preferred_element_type=jnp.float32)


def smooth_act(value):
    return value * jax.nn.sigmoid(value)


def smooth_slope(value):
    sigma = jax.nn.sigmoid(value)
    return sigma * (1.0 + value * (1.0 - sigma))


def masked_mean(values, counts):
    width = values.shape[1]
    valid_mask = lax.broadcasted_iota(jnp.int32, (values.shape[0], width), 1) < counts[:, None]
    summed = jnp.sum(jnp.where(valid_mask[:, :, None], values.astype(jnp.float32), jnp.float32(0.0)), axis=1)
    return summed / counts[:, None].astype(jnp.float32)


def upper_step(act_one, counts, targets, w2_self, w2_nbr, w3, loss_scale):
    seeds = counts.shape[0]
    hidden = act_one.shape[1]
    groups = act_one.reshape(seeds, -1, hidden)
    head_rows = groups[:, 0]
    tail_rows = groups[:, 1:]
    fan_two = tail_rows.shape[1]
    mean_two = masked_mean(tail_rows, counts).astype(jnp.bfloat16)
    pre_two = jnp.dot(head_rows, w2_self, preferred_element_type=jnp.float32) + jnp.dot(mean_two, w2_nbr, preferred_element_type=jnp.float32)
    act_two = smooth_act(pre_two).astype(jnp.bfloat16)
    logits = jnp.dot(act_two, w3, preferred_element_type=jnp.float32)
    shifted = logits - jnp.max(logits, axis=1, keepdims=True)
    expsum = jnp.exp(shifted)
    probability = expsum / jnp.sum(expsum, axis=1, keepdims=True)
    onehot = (lax.broadcasted_iota(jnp.int32, logits.shape, 1) == targets[:, None]).astype(jnp.float32)
    grad_three = ((probability - onehot) * loss_scale).astype(jnp.bfloat16)
    grad_w3 = inner_rows(act_two, grad_three)
    grad_two = (outer_cols(grad_three, w3) * smooth_slope(pre_two)).astype(jnp.bfloat16)
    grad_w2s = inner_rows(head_rows, grad_two)
    grad_w2n = inner_rows(mean_two, grad_two)
    grad_head = outer_cols(grad_two, w2_self)
    grad_mean = outer_cols(grad_two, w2_nbr)
    kept_mask = lax.broadcasted_iota(jnp.int32, (seeds, fan_two), 1) < counts[:, None]
    grad_tail = jnp.where(kept_mask[:, :, None], grad_mean[:, None, :] / counts[:, None, None].astype(jnp.float32), jnp.float32(0.0))
    grad_act = jnp.concatenate([grad_head[:, None, :], grad_tail], axis=1).reshape(-1, hidden)
    return grad_w3, grad_w2s, grad_w2n, grad_act


def reference(features, nbr_ids, nbr_counts, self_ids, seed_counts, labels, w1_self, w1_nbr, w2_self, w2_nbr, w3):
    node_rows = features.T

    def aggregate_block(block):
        block_ids, block_counts = block
        picked = jnp.take(node_rows, block_ids, axis=0)
        return masked_mean(picked, block_counts).astype(jnp.bfloat16)

    aggregated = lax.map(aggregate_block, (nbr_ids.reshape(N_BATCH, ROWS_B, FAN1), nbr_counts.reshape(N_BATCH, ROWS_B)))
    aggregated = aggregated.reshape(ROWS, -1)
    own_rows = jnp.take(node_rows, self_ids, axis=0)
    pre_one = jnp.dot(own_rows, w1_self, preferred_element_type=jnp.float32) + jnp.dot(aggregated, w1_nbr, preferred_element_type=jnp.float32)
    act_one = smooth_act(pre_one).astype(jnp.bfloat16)
    grad_w3, grad_w2s, grad_w2n, grad_act = upper_step(act_one, seed_counts, labels, w2_self, w2_nbr, w3, 1.0 / SEEDS)
    grad_one = (grad_act * smooth_slope(pre_one)).astype(jnp.bfloat16)
    grad_w1s = inner_rows(own_rows, grad_one)
    grad_w1n = inner_rows(aggregated, grad_one)
    return grad_w1s, grad_w1n, grad_w2s, grad_w2n, grad_w3
```

```python
import jax
import jax.numpy as jnp
from jax import lax
from jax.experimental import pallas as pl
from jax.experimental.pallas import tpu as pltpu
from jax.sharding import Mesh, PartitionSpec as P

NODES = 65536
COLS = 11
H = 256
C = 172
FAN1 = 15
FAN2 = 10
KEEP = 1 + FAN2
IDS = 1 + FAN1
SEEDS_B = 192
ROWS_B = SEEDS_B * KEEP
Z, Y, X, CORE = 12, 8, 4, 2
FEAT = Z * Y
BATCH = X * CORE
LOSS_SCALE = 1.0 / (SEEDS_B * BATCH)
OWN = 24
OWNERS = ROWS_B // OWN
GROUPS = 3
SLOTS = 8
SLOT_ROWS = NODES // SLOTS
WIDE = 24
PART = 104
BF16 = jnp.bfloat16
F32 = jnp.float32


def vmem():
    return pl.BlockSpec(memory_space=pltpu.VMEM)


def gather_kernel(ids_ref, x_ref, o_ref, table, own_ref, agg_ref):
    lane = lax.broadcasted_iota(jnp.int32, (1, 128), 1)

    @pl.loop(0, SLOT_ROWS // 128)
    def _(block):
        stacked = []
        for slot in range(SLOTS):
            start = pl.multiple_of(slot * SLOT_ROWS + block * 128, 128)
            stacked += [x_ref[:, pl.ds(start, 128)].astype(F32), jnp.ones((1, 128), F32), jnp.zeros((4, 128), F32)]
        turned = jnp.concatenate(stacked, 0).T
        for slot in range(SLOTS):
            start = pl.multiple_of(slot * SLOT_ROWS + block * 128, 128)
            table[pl.ds(start, 128), :] = jnp.where(lane // 16 == slot, turned, 0.0)

    table[pl.ds(NODES, 8), :] = jnp.zeros((8, 128), F32)

    @pl.loop(0, OWNERS)
    def _(owner):
        base = owner * (OWN * IDS)
        for i in range(OWN):
            group, row = i // 8, i % 8
            place = pl.ds(group * (OWNERS * 8) + owner * 8 + row, 1)
            picked = [table[pl.ds(ids_ref[base + i * IDS + j], 1), :] for j in range(IDS)]
            own_ref[place, :] = picked[0]
            terms = picked[1:]
            while len(terms) > 1:
                terms = [sum(terms[a : a + 2]) for a in range(0, len(terms), 2)]
            agg_ref[place, :] = terms[0]

    def fold(rows):
        for shift in (64, 32, 16):
            rows = rows + pltpu.roll(rows, shift, 1)
        return rows

    step = 64

    @pl.loop(0, OWNERS * 8 // step)
    def _(block):
        packed = jnp.zeros((step, 128), F32)
        for group in range(GROUPS):
            place = pl.ds(pl.multiple_of(group * (OWNERS * 8) + block * step, 8), step)
            own = fold(own_ref[place, :])
            agg = fold(agg_ref[place, :])
            mean = agg / agg[:, COLS : COLS + 1]
            both = jnp.where(lane % 32 < COLS, own, pltpu.roll(mean, COLS, 1))
            packed = jnp.where(lane // 32 == group, both, packed)
        packed = jnp.where(lane % 32 < 2 * COLS, packed, 0.0)
        o_ref[pl.ds(pl.multiple_of(block * step, step), step), :] = packed.astype(BF16)

    o_ref[pl.ds(OWNERS * 8, (FEAT - OWNERS) * 8), :] = jnp.zeros(((FEAT - OWNERS) * 8, 128), BF16)


def gather(ids, features):
    return pl.pallas_call(
        gather_kernel,
        out_shape=jax.ShapeDtypeStruct((FEAT * 8, 128), BF16),
        in_specs=[pl.BlockSpec(memory_space=pltpu.SMEM), vmem()],
        out_specs=vmem(),
        scratch_shapes=[
            pltpu.VMEM((NODES + 8, 128), F32),
            pltpu.VMEM((ROWS_B, 128), F32),
            pltpu.VMEM((ROWS_B, 128), F32),
        ],
        compiler_params=pltpu.CompilerParams(vmem_limit_bytes=50 * 1024 * 1024),
        cost_estimate=pl.CostEstimate(flops=80_000_000, bytes_accessed=150_000_000, transcendentals=0),
        name="gather",
    )(ids, features)


def project_kernel(r_ref, w_ref, o_ref):
    lane = lax.broadcasted_iota(jnp.int32, (1, 128), 1)
    total = jnp.zeros((OWN, H), F32)
    for quad in range(FEAT // 4):
        rows = r_ref[pl.ds(quad * 32, 32), :].astype(F32)
        left = []
        for group in range(GROUPS):
            mixed = jnp.zeros((8, 128), F32)
            for j in range(4):
                one = rows[j * 8 : (j + 1) * 8]
                shift = (j * WIDE - group * 32) % 128
                one = pltpu.roll(one, shift, 1) if shift else one
                mixed = jnp.where(lane // WIDE == j, one, mixed)
            left.append(mixed)
        left = jnp.concatenate(left, 0)[:, : 4 * WIDE].astype(BF16)
        right = w_ref[pl.ds(quad * 4 * WIDE, 4 * WIDE), :]
        total = total + jnp.dot(left, right, preferred_element_type=F32)
    o_ref[...] = total.astype(BF16)


def project(received, w1_all):
    return pl.pallas_call(
        project_kernel,
        out_shape=jax.ShapeDtypeStruct((OWN, H), BF16),
        in_specs=[vmem(), vmem()],
        out_specs=vmem(),
        compiler_params=pltpu.CompilerParams(vmem_limit_bytes=32 * 1024 * 1024),
        name="project",
    )(received, w1_all)


def sigmoid(value):
    return 1.0 / (1.0 + jnp.exp(-value))


def outer_cols(left, right):
    return lax.dot_general(left, right, (((1,), (1,)), ((), ())), preferred_element_type=F32)


def inner_rows(left, right):
    return lax.dot_general(left, right, (((0,), (0,)), ((), ())), preferred_element_type=F32)


def upper_kernel(z_ref, packed_ref, counts_ref, labels_ref, w2s_ref, w2n_ref, w3_ref, o_ref, g_ref):
    counts = counts_ref[...]
    scale = counts.astype(F32)
    head = None
    total = jnp.zeros((SEEDS_B, H), F32)
    for k in range(KEEP):
        value = z_ref[pl.ds(k * SEEDS_B, SEEDS_B), :].astype(F32)
        act = (value * sigmoid(value)).astype(BF16)
        if k == 0:
            head = act
        else:
            total = total + jnp.where(counts >= k, act.astype(F32), 0.0)
    mean_two = (total / scale).astype(BF16)
    pre_two = jnp.dot(head, w2s_ref[...], preferred_element_type=F32) + jnp.dot(
        mean_two, w2n_ref[...], preferred_element_type=F32
    )
    sig_two = sigmoid(pre_two)
    act_two = (pre_two * sig_two).astype(BF16)
    slope_two = sig_two * (1.0 + pre_two * (1.0 - sig_two))
    logits = jnp.dot(act_two, w3_ref[...], preferred_element_type=F32)
    expsum = jnp.exp(logits - jnp.max(logits, axis=1, keepdims=True))
    probability = expsum / jnp.sum(expsum, axis=1, keepdims=True)
    onehot = (lax.broadcasted_iota(jnp.int32, logits.shape, 1) == labels_ref[...]).astype(F32)
    grad_three = ((probability - onehot) * LOSS_SCALE).astype(BF16)
    grad_two = (outer_cols(grad_three, w3_ref[...]) * slope_two).astype(BF16)
    o_ref[pl.ds(0, H), :] = inner_rows(head, grad_two).astype(BF16)
    o_ref[pl.ds(H, H), :] = inner_rows(mean_two, grad_two).astype(BF16)
    o_ref[pl.ds(2 * H, H), :] = jnp.zeros((H, H), BF16)
    o_ref[pl.ds(2 * H, H), :C] = inner_rows(act_two, grad_three).astype(BF16)
    grad_head = outer_cols(grad_two, w2s_ref[...])
    grad_mean = outer_cols(grad_two, w2n_ref[...]) / scale
    for k in range(KEEP):
        value = z_ref[pl.ds(k * SEEDS_B, SEEDS_B), :].astype(F32)
        sig = sigmoid(value)
        slope = sig * (1.0 + value * (1.0 - sig))
        grad = grad_head if k == 0 else jnp.where(counts >= k, grad_mean, 0.0)
        grad = grad * slope
        for group in range(GROUPS):
            part = [grad[(GROUPS * a + group) * 8 :][:8] for a in range(8)]
            g_ref[group, pl.ds(k * 64, 64), :] = jnp.concatenate(part, 0).astype(BF16)
    turned = packed_ref[pl.ds(0, OWNERS * 8), :].astype(F32).T.astype(BF16)
    grad_one = jnp.zeros((32, H), F32)
    for group in range(GROUPS):
        left = turned[group * 32 : (group + 1) * 32]
        grad_one = grad_one + jnp.dot(left, g_ref[group], preferred_element_type=F32)
    o_ref[pl.ds(3 * H, 32), :] = grad_one.astype(BF16)
    rest = BATCH * PART - 3 * H - 32
    o_ref[pl.ds(3 * H + 32, rest), :] = jnp.zeros((rest, H), BF16)


def upper(pre_one, packed, counts, labels, w2_self, w2_nbr, w3):
    return pl.pallas_call(
        upper_kernel,
        out_shape=jax.ShapeDtypeStruct((BATCH * PART, H), BF16),
        in_specs=[vmem()] * 7,
        out_specs=vmem(),
        scratch_shapes=[pltpu.VMEM((GROUPS, OWNERS * 8, H), BF16)],
        compiler_params=pltpu.CompilerParams(vmem_limit_bytes=32 * 1024 * 1024),
        name="upper",
    )(pre_one, packed, counts, labels, w2_self, w2_nbr, w3)


def local(features, nbr_ids, nbr_counts, self_ids, seed_counts, labels, w1_self, w1_nbr, w2_self, w2_nbr, w3):
    w1_mine = jnp.concatenate([w1_self, w1_nbr, jnp.zeros((WIDE - 2 * COLS, H), BF16)], 0)
    w1_block = lax.all_to_all(jnp.broadcast_to(w1_mine[None], (Y, WIDE, H)), "y", 0, 0)
    w1_all = lax.all_gather(w1_block.reshape(Y * WIDE, H), "z", axis=0, tiled=True)

    valid = lax.broadcasted_iota(jnp.int32, (ROWS_B, FAN1), 1) < nbr_counts[:, None]
    ids = jnp.concatenate([self_ids[:, None], jnp.where(valid, nbr_ids, NODES)], 1)
    ids = ids.reshape(SEEDS_B, KEEP, IDS).transpose(1, 0, 2).reshape(-1)
    packed = gather(ids, features)

    received = lax.all_to_all(packed.reshape(FEAT, 8, 128), ("z", "y"), 0, 0)
    pre_mine = project(received.reshape(FEAT * 8, 128), w1_all)
    pre_one = lax.all_to_all(jnp.broadcast_to(pre_mine[None], (FEAT, OWN, H)), ("z", "y"), 0, 0)
    grads = upper(
        pre_one.reshape(FEAT * OWN, H), packed, seed_counts[:, None], labels[:, None], w2_self, w2_nbr, w3
    )
    shares = lax.all_to_all(grads.reshape(BATCH, PART, H), ("x", "core"), 0, 0)
    summed = jnp.sum(shares.astype(F32), axis=0)
    whole = lax.all_gather(summed, ("x", "core"), axis=0, tiled=True)
    first = 3 * H
    return (
        whole[first : first + COLS],
        whole[first + COLS : first + 2 * COLS],
        whole[:H],
        whole[H : 2 * H],
        whole[2 * H : 3 * H, :C],
    )


def solution(mesh):
    split = Mesh(mesh.devices.reshape(Z, Y, X, CORE), ("z", "y", "x", "core"))
    feat, batch = P(("z", "y"), None), P(("x", "core"))
    in_specs = (feat, P(("x", "core"), None), batch, batch, batch, batch, feat, feat, P(), P(), P())
    out_specs = (feat, feat, P(), P(), P())
    return jax.shard_map(local, mesh=split, in_specs=in_specs, out_specs=out_specs, check_vma=False)
```

```python
import jax
import jax.numpy as jnp
from jax import lax
from jax.experimental import pallas as pl
from jax.experimental.pallas import tpu as pltpu
from jax.sharding import Mesh, PartitionSpec as P

NODES = 65536
COLS = 11
H = 256
C = 172
FAN1 = 15
FAN2 = 10
IDS = 1 + FAN1
KEEP = 1 + FAN2
SEEDS_B = 192
ROWS_B = SEEDS_B * KEEP
Z, Y, X, CORE = 12, 8, 4, 2
BATCH = X * CORE
LOSS_SCALE = 1.0 / (SEEDS_B * BATCH)
SEEDS_Y = SEEDS_B // Y
ROWS_Y = SEEDS_Y * KEEP
GROUPS = 3
PACKED = ROWS_Y // GROUPS
SLOTS = 8
SLOT_ROWS = NODES // SLOTS
CHUNK = 128
LANES = -(-ROWS_B // CHUNK) * CHUNK
WIDE = 24
SEND = 144
SHARE = 24
ROWS_Z = Z * SHARE
BACK = 32 + 2 * SEEDS_Y
PART = 104
BF16 = jnp.bfloat16
F32 = jnp.float32
VMEM = pl.BlockSpec(memory_space=pltpu.VMEM)
SMEM = pl.BlockSpec(memory_space=pltpu.SMEM)


def gather_kernel(self_ref, nbr_ref, counts_ref, x_ref, w1s_ref, w1n_ref, o_ref, table, own_ref, agg_ref, stage, ids, near, sems):
    lane = lax.broadcasted_iota(jnp.int32, (1, 128), 1)

    def fetch(chunk, slot):
        at = chunk * CHUNK if isinstance(chunk, int) else pl.multiple_of(chunk * CHUNK, CHUNK)
        return pltpu.make_async_copy(ids.at[:, pl.ds(at, CHUNK)], near[slot], sems.at[slot])

    last = LANES - CHUNK
    ids[:, pl.ds(last, CHUNK)] = jnp.zeros((IDS, CHUNK), jnp.int32)
    valid = lax.broadcasted_iota(jnp.int32, (FAN1, ROWS_B), 0) < counts_ref[...]
    ids[pl.ds(0, FAN1), pl.ds(0, ROWS_B)] = jnp.where(valid, nbr_ref[...], NODES)
    ids[pl.ds(FAN1, 1), pl.ds(0, ROWS_B)] = self_ref[...]
    for slot in range(2):
        fetch(slot, slot).start()

    @pl.loop(0, SLOT_ROWS // 128, unroll=2)
    def _(block):
        stacked = []
        for slot in range(SLOTS):
            start = pl.multiple_of(slot * SLOT_ROWS + block * 128, 128)
            stacked += [x_ref[:, pl.ds(start, 128)].astype(F32), jnp.ones((1, 128), F32), jnp.zeros((4, 128), F32)]
        turned = jnp.concatenate(stacked, 0).T
        for slot in range(SLOTS):
            start = pl.multiple_of(slot * SLOT_ROWS + block * 128, 128)
            table[pl.ds(start, 128), :] = jnp.where(lane // 16 == slot, turned, 0.0)

    table[pl.ds(NODES, 8), :] = jnp.zeros((8, 128), F32)

    def take(chunk, slot, targets):
        first = chunk * CHUNK
        for i in range(targets):
            own_ref[pl.ds(first + i, 1), :] = table[pl.ds(near[slot][FAN1, i], 1), :]
            terms = [table[pl.ds(near[slot][j, i], 1), :] for j in range(FAN1)]
            while len(terms) > 1:
                terms = [sum(terms[a : a + 2]) for a in range(0, len(terms), 2)]
            agg_ref[pl.ds(first + i, 1), :] = terms[0]

    whole = ROWS_B // CHUNK

    @pl.loop(0, whole // 2)
    def _(pair):
        for slot in range(2):
            chunk = pair * 2 + slot
            fetch(chunk, slot).wait()
            take(chunk, slot, CHUNK)

            @pl.when(chunk + 2 <= whole)
            def _():
                fetch(chunk + 2, slot).start()

    fetch(whole, 0).wait()
    take(whole, 0, ROWS_B - whole * CHUNK)

    def halves(low, high, width):
        mask = lane % (2 * width) < width
        if high is None:
            return jnp.where(mask, low + pltpu.roll(low, 128 - width, 1), 0.0)
        moved = jnp.where(mask, pltpu.roll(low, 128 - width, 1), pltpu.roll(high, width, 1))
        return jnp.where(mask, low, high) + moved

    @pl.loop(0, Y)
    def _(block):
        for step in range(PACKED // 8):
            v = []
            for group in range(GROUPS):
                place = pl.ds(pl.multiple_of(block * ROWS_Y + group * PACKED + step * 8, 8), 8)
                v += [own_ref[place, :], agg_ref[place, :]]
            v = [halves(v[q], v[q + 4] if q < 2 else None, 64) for q in range(4)]
            v = [halves(v[q], v[q + 2], 32) for q in range(2)]
            stage[pl.ds(pl.multiple_of(block * SEND + step * 8, 8), 8), :] = halves(v[0], v[1], 16)

    w1 = jnp.concatenate([w1s_ref[...].astype(F32), w1n_ref[...].astype(F32), jnp.zeros((WIDE - 2 * COLS, H), F32)], 0)
    row = lax.broadcasted_iota(jnp.int32, (128, 128), 0)
    column = lax.broadcasted_iota(jnp.int32, (128, 128), 1)
    counter = jnp.where((row % 16 == COLS) & (row // 16 == column // 16), 1.0, 0.0).astype(BF16)

    @pl.loop(0, Y)
    def _(block):
        first = pl.multiple_of(block * SEND, 16)
        packed = stage[pl.ds(first, PACKED), :]
        counted = jnp.dot(packed.astype(BF16), counter, preferred_element_type=F32)
        packed = jnp.where((lane < GROUPS * 32) & (lane % 16 < COLS), packed / counted, 0.0)
        rest = jnp.zeros((SEND - PACKED - 2 * WIDE, 128), F32)
        message = jnp.concatenate([packed, w1[:, :128], w1[:, 128:], rest], 0)
        o_ref[pl.ds(first, SEND), :] = message.astype(BF16)


def gather(self_ids, nbr_ids, counts, features, w1_self, w1_nbr):
    return pl.pallas_call(
        gather_kernel,
        out_shape=jax.ShapeDtypeStruct((Y * SEND, 128), BF16),
        in_specs=[VMEM] * 6,
        out_specs=VMEM,
        scratch_shapes=[
            pltpu.VMEM((NODES + 8, 128), F32),
            pltpu.VMEM((ROWS_B, 128), F32),
            pltpu.VMEM((ROWS_B, 128), F32),
            pltpu.VMEM((Y * SEND, 128), F32),
            pltpu.VMEM((IDS, LANES), jnp.int32),
            [pltpu.SMEM((IDS, CHUNK), jnp.int32)] * 2,
            pltpu.SemaphoreType.DMA((2,)),
        ],
        compiler_params=pltpu.CompilerParams(vmem_limit_bytes=50 * 1024 * 1024),
        name="gather",
    )(self_ids, nbr_ids, counts, features, w1_self, w1_nbr)


def project_kernel(r_ref, o_ref, left_ref):
    lane = lax.broadcasted_iota(jnp.int32, (1, 128), 1)
    blocks = [r_ref[pl.ds(y * SEND, SEND), :].astype(F32) for y in range(Y)]
    right = []
    gap = jnp.zeros((16 - COLS, H), F32)
    for block in blocks:
        rows = jnp.concatenate([block[PACKED + half * WIDE :][:WIDE] for half in range(2)], 1)
        right += [rows[:COLS], gap, rows[COLS : 2 * COLS], gap]
    right = jnp.concatenate(right, 0).astype(BF16)
    left = []
    for group in range(GROUPS):
        halves = []
        for half in range(2):
            mixed = jnp.zeros((PACKED, 128), F32)
            for j in range(4):
                one = blocks[half * 4 + j][:PACKED]
                shift = (j - group) * 32 % 128
                one = pltpu.roll(one, shift, 1) if shift else one
                mixed = jnp.where(lane // 32 == j, one, mixed)
            halves.append(mixed)
        left.append(jnp.concatenate(halves, 1))
    left = jnp.concatenate(left, 0).astype(BF16)
    left_ref[...] = left
    total = jnp.dot(left, right, preferred_element_type=F32)
    o_ref[...] = jnp.concatenate([total, jnp.zeros((ROWS_Z - ROWS_Y, H), F32)], 0).astype(BF16)


def project(received):
    return pl.pallas_call(
        project_kernel,
        out_shape=(jax.ShapeDtypeStruct((ROWS_Z, H), BF16), jax.ShapeDtypeStruct((ROWS_Y, Y * 32), BF16)),
        in_specs=[VMEM],
        out_specs=(VMEM, VMEM),
        compiler_params=pltpu.CompilerParams(vmem_limit_bytes=32 * 1024 * 1024),
        name="project",
    )(received)


def spread_kernel(s_ref, o_ref):
    total = jnp.zeros((SHARE, H), F32)
    for pair in range(Z // 2):
        both = s_ref[pl.ds(pair * 2 * SHARE, 2 * SHARE), :].astype(F32)
        total = total + (both[:SHARE] + both[SHARE:])
    twice = jnp.concatenate([total, total], 0).astype(BF16)
    for pair in range(Z // 2):
        o_ref[pl.ds(pair * 2 * SHARE, 2 * SHARE), :] = twice


def spread(shares):
    return pl.pallas_call(
        spread_kernel,
        out_shape=jax.ShapeDtypeStruct((ROWS_Z, H), BF16),
        in_specs=[VMEM],
        out_specs=VMEM,
        name="spread",
    )(shares)


def sigmoid(value):
    return 1.0 / (1.0 + jnp.exp(-value))


def outer_cols(left, right):
    return lax.dot_general(left, right, (((1,), (1,)), ((), ())), preferred_element_type=F32)


def inner_rows(left, right):
    return lax.dot_general(left, right, (((0,), (0,)), ((), ())), preferred_element_type=F32)


def top(head, mean_two, labels, w2_self, w2_nbr, w3):
    pre_two = jnp.dot(head, w2_self, preferred_element_type=F32) + jnp.dot(mean_two, w2_nbr, preferred_element_type=F32)
    sig_two = sigmoid(pre_two)
    act_two = (pre_two * sig_two).astype(BF16)
    slope_two = sig_two * (1.0 + pre_two * (1.0 - sig_two))
    logits = jnp.dot(act_two, w3, preferred_element_type=F32)
    expsum = jnp.exp(logits - jnp.max(logits, axis=1, keepdims=True))
    probability = expsum / jnp.sum(expsum, axis=1, keepdims=True)
    onehot = (lax.broadcasted_iota(jnp.int32, logits.shape, 1) == labels).astype(F32)
    grad_three = ((probability - onehot) * LOSS_SCALE).astype(BF16)
    grad_two = (outer_cols(grad_three, w3) * slope_two).astype(BF16)
    return act_two, grad_three, grad_two


def seeds_kernel(place_ref, z_ref, left_ref, counts_ref, labels_ref, w2s_ref, w2n_ref, w3_ref, o_ref, stage):
    mine = pl.ds(pl.multiple_of(place_ref[0] * SEEDS_Y, 8), SEEDS_Y)
    counts = counts_ref[mine, :]
    scale = counts.astype(F32)
    pre_one = z_ref[...].astype(F32)[:ROWS_Y]
    sig_one = sigmoid(pre_one)
    act_one = (pre_one * sig_one).astype(BF16)
    slope_one = sig_one * (1.0 + pre_one * (1.0 - sig_one))
    behind = lax.broadcasted_iota(jnp.int32, (SEEDS_Y, ROWS_Y), 1) - KEEP * lax.broadcasted_iota(jnp.int32, (SEEDS_Y, ROWS_Y), 0)

    def choose(mask):
        return jnp.where(mask, 1.0, 0.0).astype(BF16)

    kept = choose((behind > 0) & (behind <= counts))
    belongs = choose((behind >= 0) & (behind < KEEP))
    is_head = choose(behind == 0)
    head = jnp.dot(is_head, act_one, preferred_element_type=F32).astype(BF16)
    mean_two = (jnp.dot(kept, act_one, preferred_element_type=F32) / scale).astype(BF16)
    _, _, grad_two = top(head, mean_two, labels_ref[mine, :], w2s_ref[...], w2n_ref[...], w3_ref[...])
    ones = jnp.ones((SEEDS_Y, H), BF16)
    grad_rows = inner_rows(belongs, grad_two).astype(BF16)
    scale_rows = inner_rows(belongs, (ones * scale).astype(BF16))
    grad_mean = outer_cols(grad_rows, w2n_ref[...]) / scale_rows
    grad = jnp.where(inner_rows(kept, ones) > 0.5, grad_mean, 0.0)
    grad = jnp.where(inner_rows(is_head, ones) > 0.5, outer_cols(grad_rows, w2s_ref[...]), grad)
    grad_one = inner_rows(left_ref[...], (grad * slope_one).astype(BF16))
    for y in range(Y):
        stage[pl.ds(y * BACK, 32), :] = grad_one[y * 32 :][:32]
        stage[pl.ds(y * BACK + 32, SEEDS_Y), :] = head.astype(F32)
        stage[pl.ds(y * BACK + 32 + SEEDS_Y, SEEDS_Y), :] = mean_two.astype(F32)
    o_ref[...] = stage[...].astype(BF16)


def seeds(place, pre_one, left, counts, labels, w2_self, w2_nbr, w3):
    return pl.pallas_call(
        seeds_kernel,
        out_shape=jax.ShapeDtypeStruct((Y * BACK, H), BF16),
        in_specs=[SMEM] + [VMEM] * 7,
        out_specs=VMEM,
        scratch_shapes=[pltpu.VMEM((Y * BACK, H), F32)],
        compiler_params=pltpu.CompilerParams(vmem_limit_bytes=32 * 1024 * 1024),
        name="seeds",
    )(place, pre_one, left, counts, labels, w2_self, w2_nbr, w3)


def weights_kernel(r_ref, labels_ref, w2s_ref, w2n_ref, w3_ref, o_ref):
    rows = r_ref[...].astype(F32)
    grad_one = jnp.zeros((32, H), F32)
    head, mean_two = [], []
    for y in range(Y):
        grad_one = grad_one + rows[y * BACK :][:32]
        head.append(rows[y * BACK + 32 :][:SEEDS_Y])
        mean_two.append(rows[y * BACK + 32 + SEEDS_Y :][:SEEDS_Y])
    head = jnp.concatenate(head, 0).astype(BF16)
    mean_two = jnp.concatenate(mean_two, 0).astype(BF16)
    act_two, grad_three, grad_two = top(head, mean_two, labels_ref[...], w2s_ref[...], w2n_ref[...], w3_ref[...])
    o_ref[pl.ds(0, H), :] = inner_rows(head, grad_two).astype(BF16)
    o_ref[pl.ds(H, H), :] = inner_rows(mean_two, grad_two).astype(BF16)
    o_ref[pl.ds(2 * H, H), :] = jnp.zeros((H, H), BF16)
    o_ref[pl.ds(2 * H, H), :C] = inner_rows(act_two, grad_three).astype(BF16)
    rest = BATCH * PART - 3 * H
    o_ref[pl.ds(3 * H, rest), :] = jnp.concatenate([grad_one, jnp.zeros((rest - 32, H), F32)], 0).astype(BF16)


def weights(received, labels, w2_self, w2_nbr, w3):
    return pl.pallas_call(
        weights_kernel,
        out_shape=jax.ShapeDtypeStruct((BATCH * PART, H), BF16),
        in_specs=[VMEM] * 5,
        out_specs=VMEM,
        compiler_params=pltpu.CompilerParams(vmem_limit_bytes=32 * 1024 * 1024),
        name="weights",
    )(received, labels, w2_self, w2_nbr, w3)


def exchange(rows, axis, parts):
    received = lax.all_to_all(rows.reshape(parts, -1, rows.shape[1]), axis, 0, 0)
    return received.reshape(rows.shape)


def local(features, nbr_ids, nbr_counts, self_ids, seed_counts, labels, w1_self, w1_nbr, w2_self, w2_nbr, w3):
    packed = gather(self_ids[None], nbr_ids.T, nbr_counts[None], features, w1_self, w1_nbr)
    shares, left = project(exchange(packed, "y", Y))
    pre_one = exchange(spread(exchange(shares, "z", Z)), "z", Z)
    place = lax.axis_index("y").astype(jnp.int32)[None]
    labels = labels[:, None]
    back = seeds(place, pre_one, left, seed_counts[:, None], labels, w2_self, w2_nbr, w3)
    grads = weights(exchange(back, "y", Y), labels, w2_self, w2_nbr, w3)
    grads = lax.all_to_all(grads.reshape(BATCH, PART, H), ("x", "core"), 0, 0)
    summed = jnp.sum(grads.astype(F32), axis=0)
    whole = lax.all_gather(summed, ("x", "core"), axis=0, tiled=True)
    first = 3 * H
    return (
        whole[first : first + COLS],
        whole[first + 16 : first + 16 + COLS],
        whole[:H],
        whole[H : 2 * H],
        whole[2 * H : 3 * H, :C],
    )


def solution(mesh):
    split = Mesh(mesh.devices.reshape(Z, Y, X, CORE), ("z", "y", "x", "core"))
    feat, batch = P(("z", "y"), None), P(("x", "core"))
    in_specs = (feat, P(("x", "core"), None), batch, batch, batch, batch, feat, feat, P(), P(), P())
    out_specs = (feat, feat, P(), P(), P())
    return jax.shard_map(local, mesh=split, in_specs=in_specs, out_specs=out_specs, check_vma=False)
```

```python
import jax
import jax.numpy as jnp
from jax import lax
from jax.experimental import pallas as pl
from jax.experimental.pallas import tpu as pltpu
from jax.sharding import Mesh, PartitionSpec as P

NODES = 65536
COLS = 11
H = 256
C = 172
FAN1 = 15
FAN2 = 10
IDS = 1 + FAN1
KEEP = 1 + FAN2
SEEDS_B = 192
ROWS_B = SEEDS_B * KEEP
Z, Y, X, CORE = 12, 8, 4, 2
BATCH = X * CORE
LOSS_SCALE = 1.0 / (SEEDS_B * BATCH)
SEEDS_Y = SEEDS_B // Y
ROWS_Y = SEEDS_Y * KEEP
GROUPS = 3
PACKED = ROWS_Y // GROUPS
SLOTS = 8
SLOT_ROWS = NODES // SLOTS
CHUNK = 64
CHUNKS = ROWS_B // CHUNK
AHEAD = 4
WIDE = 24
SEND = 144
SHARE = 24
ROWS_Z = Z * SHARE
BACK = 32 + 2 * SEEDS_Y
AT_FIRST = 2 * H
AT_THIRD = AT_FIRST + 32
HALF = 368
PIECES = 4
BF16 = jnp.bfloat16
F32 = jnp.float32
VMEM = pl.BlockSpec(memory_space=pltpu.VMEM)
SMEM = pl.BlockSpec(memory_space=pltpu.SMEM)
HBM = pl.BlockSpec(memory_space=pltpu.HBM)


def gather_kernel(
    self_in, nbr_in, counts_in, x_in, w1s_in, w1n_in, o_ref,
    self_ref, nbr_ref, counts_ref, x_ref, w1s_ref, w1n_ref, small_sems, x_sems,
    table, own_ref, agg_ref, stage, ids, near, sems,
):
    lane = lax.broadcasted_iota(jnp.int32, (1, 128), 1)
    small = [(self_in, self_ref), (nbr_in, nbr_ref), (counts_in, counts_ref), (w1s_in, w1s_ref), (w1n_in, w1n_ref)]
    small = [pltpu.make_async_copy(source, target, small_sems.at[i]) for i, (source, target) in enumerate(small)]
    for copy in small:
        copy.start()
    pieces = []
    for piece in range(PIECES):
        pieces.append([])
        for slot in range(SLOTS):
            place = pl.ds(slot * SLOT_ROWS + piece * (SLOT_ROWS // PIECES), SLOT_ROWS // PIECES)
            pieces[piece].append(pltpu.make_async_copy(x_in.at[:, place], x_ref.at[:, place], x_sems.at[piece, slot]))
            pieces[piece][slot].start()
    def fetch(chunk, slot):
        return pltpu.make_async_copy(ids.at[chunk], near[slot], sems.at[slot])

    def tabulate(piece):
        for copy in pieces[piece]:
            copy.wait()

        @pl.loop(0, SLOT_ROWS // PIECES // 128, unroll=4)
        def _(step):
            block = step + piece * (SLOT_ROWS // PIECES // 128)
            stacked = []
            for slot in range(SLOTS):
                start = pl.multiple_of(slot * SLOT_ROWS + block * 128, 128)
                stacked += [x_ref[:, pl.ds(start, 128)].astype(F32), jnp.ones((1, 128), F32), jnp.zeros((4, 128), F32)]
            turned = jnp.concatenate(stacked, 0).astype(BF16).T.astype(F32)
            for slot in range(SLOTS):
                start = pl.multiple_of(slot * SLOT_ROWS + block * 128, 128)
                table[pl.ds(start, 128), :] = jnp.where(lane // 16 == slot, turned, 0.0)

    tabulate(0)
    for copy in small:
        copy.wait()
    counts = counts_ref[...][None, :]
    valid = lax.broadcasted_iota(jnp.int32, (FAN1, ROWS_B), 0) < counts
    both = jnp.concatenate([jnp.where(valid, nbr_ref[...], NODES), self_ref[...][None, :]], 0)
    both = jnp.concatenate([both, jnp.zeros((IDS, CHUNK), jnp.int32)], 1)
    for tile in range(-(-ROWS_B // 128)):
        low, high = both[:8, tile * 128 :][:, :128], both[8:, tile * 128 :][:, :128]
        ids[2 * tile] = jnp.where(lane < CHUNK, low, pltpu.roll(high, CHUNK, 1))
        if 2 * tile + 1 < CHUNKS:
            ids[2 * tile + 1] = jnp.where(lane < CHUNK, pltpu.roll(low, CHUNK, 1), high)
    for slot in range(AHEAD):
        fetch(slot, slot).start()
    for piece in range(1, PIECES):
        tabulate(piece)
    table[pl.ds(NODES, 8), :] = jnp.zeros((8, 128), F32)

    def take(chunk, slot):
        fetch(chunk, slot).wait()
        first = chunk * CHUNK
        for i in range(CHUNK):
            rows = [table[pl.ds(near[slot][j % 8, j // 8 * CHUNK + i], 1), :] for j in range(IDS)]
            own_ref[pl.ds(first + i, 1), :] = rows.pop()
            while len(rows) > 1:
                rows = [sum(rows[a : a + 2]) for a in range(0, len(rows), 2)]
            agg_ref[pl.ds(first + i, 1), :] = rows[0]

    @pl.loop(0, CHUNKS // AHEAD)
    def _(turn):
        for slot in range(AHEAD):
            chunk = turn * AHEAD + slot
            take(chunk, slot)

            @pl.when(chunk + AHEAD < CHUNKS)
            def _():
                fetch(chunk + AHEAD, slot).start()

    for slot in range(CHUNKS % AHEAD):
        take(CHUNKS // AHEAD * AHEAD + slot, slot)

    def halves(low, high, width):
        mask = lane % (2 * width) < width
        if high is None:
            return jnp.where(mask, low + pltpu.roll(low, 128 - width, 1), 0.0)
        moved = jnp.where(mask, pltpu.roll(low, 128 - width, 1), pltpu.roll(high, width, 1))
        return jnp.where(mask, low, high) + moved

    @pl.loop(0, Y)
    def _(block):
        for step in range(PACKED // 8):
            v = []
            for group in range(GROUPS):
                place = pl.ds(pl.multiple_of(block * ROWS_Y + group * PACKED + step * 8, 8), 8)
                v += [own_ref[place, :], agg_ref[place, :]]
            v = [halves(v[q], v[q + 4] if q < 2 else None, 64) for q in range(4)]
            v = [halves(v[q], v[q + 2], 32) for q in range(2)]
            stage[pl.ds(pl.multiple_of(block * SEND + step * 8, 8), 8), :] = halves(v[0], v[1], 16)

    w1 = jnp.concatenate([w1s_ref[...].astype(F32), w1n_ref[...].astype(F32), jnp.zeros((WIDE - 2 * COLS, H), F32)], 0)
    row = lax.broadcasted_iota(jnp.int32, (128, 128), 0)
    column = lax.broadcasted_iota(jnp.int32, (128, 128), 1)
    counter = jnp.where((row % 16 == COLS) & (row // 16 == column // 16), 1.0, 0.0).astype(BF16)

    @pl.loop(0, Y)
    def _(block):
        first = pl.multiple_of(block * SEND, 16)
        packed = stage[pl.ds(first, PACKED), :]
        counted = jnp.dot(packed.astype(BF16), counter, preferred_element_type=F32)
        packed = jnp.where((lane < GROUPS * 32) & (lane % 16 < COLS), packed / counted, 0.0)
        rest = jnp.zeros((SEND - PACKED - 2 * WIDE, 128), F32)
        message = jnp.concatenate([packed, w1[:, :128], w1[:, 128:], rest], 0)
        o_ref[pl.ds(first, SEND), :] = message.astype(BF16)


def gather(self_ids, nbr_ids, counts, features, w1_self, w1_nbr):
    return pl.pallas_call(
        gather_kernel,
        out_shape=jax.ShapeDtypeStruct((Y * SEND, 128), BF16),
        in_specs=[HBM] * 6,
        out_specs=VMEM,
        scratch_shapes=[
            pltpu.VMEM((ROWS_B,), jnp.int32),
            pltpu.VMEM((FAN1, ROWS_B), jnp.int32),
            pltpu.VMEM((ROWS_B,), jnp.int32),
            pltpu.VMEM((COLS, NODES), BF16),
            pltpu.VMEM((COLS, H), BF16),
            pltpu.VMEM((COLS, H), BF16),
            pltpu.SemaphoreType.DMA((5,)),
            pltpu.SemaphoreType.DMA((PIECES, SLOTS)),
            pltpu.VMEM((NODES + 8, 128), F32),
            pltpu.VMEM((ROWS_B, 128), F32),
            pltpu.VMEM((ROWS_B, 128), F32),
            pltpu.VMEM((Y * SEND, 128), F32),
            pltpu.VMEM((CHUNKS, 8, 128), jnp.int32),
            [pltpu.SMEM((8, 128), jnp.int32)] * AHEAD,
            pltpu.SemaphoreType.DMA((AHEAD,)),
        ],
        compiler_params=pltpu.CompilerParams(vmem_limit_bytes=63 * 1024 * 1024),
        name="gather",
    )(self_ids, nbr_ids, counts, features, w1_self, w1_nbr)


def project_kernel(r_ref, o_ref, left_ref):
    lane = lax.broadcasted_iota(jnp.int32, (1, 128), 1)
    blocks = [r_ref[pl.ds(y * SEND, SEND), :].astype(F32) for y in range(Y)]
    right = []
    gap = jnp.zeros((16 - COLS, H), F32)
    for block in blocks:
        rows = jnp.concatenate([block[PACKED + half * WIDE :][:WIDE] for half in range(2)], 1)
        right += [rows[:COLS], gap, rows[COLS : 2 * COLS], gap]
    right = jnp.concatenate(right, 0).astype(BF16)
    left = []
    for group in range(GROUPS):
        halves = []
        for half in range(2):
            mixed = jnp.zeros((PACKED, 128), F32)
            for j in range(4):
                one = blocks[half * 4 + j][:PACKED]
                shift = (j - group) * 32 % 128
                one = pltpu.roll(one, shift, 1) if shift else one
                mixed = jnp.where(lane // 32 == j, one, mixed)
            halves.append(mixed)
        left.append(jnp.concatenate(halves, 1))
    left = jnp.concatenate(left, 0).astype(BF16)
    left_ref[...] = left
    total = jnp.dot(left, right, preferred_element_type=F32)
    o_ref[...] = jnp.concatenate([total, jnp.zeros((ROWS_Z - ROWS_Y, H), F32)], 0).astype(BF16)


def project(received):
    return pl.pallas_call(
        project_kernel,
        out_shape=(jax.ShapeDtypeStruct((ROWS_Z, H), BF16), jax.ShapeDtypeStruct((ROWS_Y, Y * 32), BF16)),
        in_specs=[VMEM],
        out_specs=(VMEM, VMEM),
        compiler_params=pltpu.CompilerParams(vmem_limit_bytes=32 * 1024 * 1024),
        name="project",
    )(received)


def spread_kernel(s_ref, o_ref):
    total = jnp.zeros((SHARE, H), F32)
    for pair in range(Z // 2):
        both = s_ref[pl.ds(pair * 2 * SHARE, 2 * SHARE), :].astype(F32)
        total = total + (both[:SHARE] + both[SHARE:])
    twice = jnp.concatenate([total, total], 0).astype(BF16)
    for pair in range(Z // 2):
        o_ref[pl.ds(pair * 2 * SHARE, 2 * SHARE), :] = twice


def spread(shares):
    return pl.pallas_call(
        spread_kernel,
        out_shape=jax.ShapeDtypeStruct((ROWS_Z, H), BF16),
        in_specs=[VMEM],
        out_specs=VMEM,
        compiler_params=pltpu.CompilerParams(vmem_limit_bytes=16 * 1024 * 1024),
        name="spread",
    )(shares)


def sigmoid(value):
    return 1.0 / (1.0 + jnp.exp(-value))


def outer_cols(left, right):
    return lax.dot_general(left, right, (((1,), (1,)), ((), ())), preferred_element_type=F32)


def inner_rows(left, right):
    return lax.dot_general(left, right, (((0,), (0,)), ((), ())), preferred_element_type=F32)


def top(head, mean_two, labels, w2_self, w2_nbr, w3):
    pre_two = jnp.dot(head, w2_self, preferred_element_type=F32) + jnp.dot(mean_two, w2_nbr, preferred_element_type=F32)
    sig_two = sigmoid(pre_two)
    act_two = (pre_two * sig_two).astype(BF16)
    slope_two = sig_two * (1.0 + pre_two * (1.0 - sig_two))
    logits = outer_cols(act_two, w3)
    expsum = jnp.exp(logits - jnp.max(logits, axis=1, keepdims=True))
    probability = expsum / jnp.sum(expsum, axis=1, keepdims=True)
    onehot = (lax.broadcasted_iota(jnp.int32, logits.shape, 1) == labels).astype(F32)
    grad_three = ((probability - onehot) * LOSS_SCALE).astype(BF16)
    grad_two = (jnp.dot(grad_three, w3, preferred_element_type=F32) * slope_two).astype(BF16)
    return act_two, grad_three, grad_two


def as_column(ref, first, rows):
    row = lax.broadcasted_iota(jnp.int32, (rows, SEEDS_B), 0) + first
    column = lax.broadcasted_iota(jnp.int32, (rows, SEEDS_B), 1)
    spread_out = jnp.where(row == column, ref[...][None, :], 0).astype(F32)
    return jnp.sum(spread_out, axis=1, keepdims=True).astype(jnp.int32)


def seeds_kernel(place_ref, z_ref, left_ref, counts_ref, labels_ref, w2s_ref, w2n_ref, w3_ref, o_ref, stage):
    first = place_ref[0] * SEEDS_Y
    counts = as_column(counts_ref, first, SEEDS_Y)
    scale = counts.astype(F32)
    pre_one = z_ref[...].astype(F32)[:ROWS_Y]
    sig_one = sigmoid(pre_one)
    act_one = (pre_one * sig_one).astype(BF16)
    slope_one = sig_one * (1.0 + pre_one * (1.0 - sig_one))
    behind = lax.broadcasted_iota(jnp.int32, (SEEDS_Y, ROWS_Y), 1) - KEEP * lax.broadcasted_iota(jnp.int32, (SEEDS_Y, ROWS_Y), 0)

    def choose(mask):
        return jnp.where(mask, 1.0, 0.0).astype(BF16)

    kept = choose((behind > 0) & (behind <= counts))
    belongs = choose((behind >= 0) & (behind < KEEP))
    is_head = choose(behind == 0)
    head = jnp.dot(is_head, act_one, preferred_element_type=F32).astype(BF16)
    mean_two = (jnp.dot(kept, act_one, preferred_element_type=F32) / scale).astype(BF16)
    _, _, grad_two = top(head, mean_two, as_column(labels_ref, first, SEEDS_Y), w2s_ref[...], w2n_ref[...], w3_ref[...])
    ones = jnp.ones((SEEDS_Y, H), BF16)
    grad_rows = inner_rows(belongs, grad_two).astype(BF16)
    scale_rows = inner_rows(belongs, (ones * scale).astype(BF16))
    grad_mean = outer_cols(grad_rows, w2n_ref[...]) / scale_rows
    grad = jnp.where(inner_rows(kept, ones) > 0.5, grad_mean, 0.0)
    grad = jnp.where(inner_rows(is_head, ones) > 0.5, outer_cols(grad_rows, w2s_ref[...]), grad)
    grad_one = inner_rows(left_ref[...], (grad * slope_one).astype(BF16))
    for y in range(Y):
        stage[pl.ds(y * BACK, 32), :] = grad_one[y * 32 :][:32]
        stage[pl.ds(y * BACK + 32, SEEDS_Y), :] = head.astype(F32)
        stage[pl.ds(y * BACK + 32 + SEEDS_Y, SEEDS_Y), :] = mean_two.astype(F32)
    o_ref[...] = stage[...].astype(BF16)


def seeds(place, pre_one, left, counts, labels, w2_self, w2_nbr, w3):
    return pl.pallas_call(
        seeds_kernel,
        out_shape=jax.ShapeDtypeStruct((Y * BACK, H), BF16),
        in_specs=[SMEM] + [VMEM] * 7,
        out_specs=VMEM,
        scratch_shapes=[pltpu.VMEM((Y * BACK, H), F32)],
        compiler_params=pltpu.CompilerParams(vmem_limit_bytes=32 * 1024 * 1024),
        name="seeds",
    )(place, pre_one, left, counts, labels, w2_self, w2_nbr, w3)


def weights_kernel(r_ref, labels_ref, w2s_ref, w2n_ref, w3_ref, o_ref):
    rows = r_ref[...].astype(F32)
    grad_one = jnp.zeros((32, H), F32)
    head, mean_two = [], []
    for y in range(Y):
        grad_one = grad_one + rows[y * BACK :][:32]
        head.append(rows[y * BACK + 32 :][:SEEDS_Y])
        mean_two.append(rows[y * BACK + 32 + SEEDS_Y :][:SEEDS_Y])
    head = jnp.concatenate(head, 0).astype(BF16)
    mean_two = jnp.concatenate(mean_two, 0).astype(BF16)
    act_two, grad_three, grad_two = top(head, mean_two, as_column(labels_ref, 0, SEEDS_B), w2s_ref[...], w2n_ref[...], w3_ref[...])
    o_ref[pl.ds(0, H), :] = inner_rows(head, grad_two)
    o_ref[pl.ds(H, H), :] = inner_rows(mean_two, grad_two)
    o_ref[pl.ds(AT_FIRST, 32), :] = grad_one
    o_ref[pl.ds(AT_THIRD, C), :] = inner_rows(grad_three, act_two)
    rest = 2 * HALF - AT_THIRD - C
    o_ref[pl.ds(AT_THIRD + C, rest), :] = jnp.zeros((rest, H), F32)


def weights(received, labels, w2_self, w2_nbr, w3):
    return pl.pallas_call(
        weights_kernel,
        out_shape=jax.ShapeDtypeStruct((2 * HALF, H), F32),
        in_specs=[VMEM] * 5,
        out_specs=VMEM,
        compiler_params=pltpu.CompilerParams(vmem_limit_bytes=32 * 1024 * 1024),
        name="weights",
    )(received, labels, w2_self, w2_nbr, w3)


def halve_kernel(g_ref, o_ref):
    total = (g_ref[pl.ds(0, HALF), :] + g_ref[pl.ds(HALF, HALF), :]).astype(BF16)
    for x in range(X):
        o_ref[pl.ds(x * HALF, HALF), :] = total


def halve(received):
    return pl.pallas_call(
        halve_kernel,
        out_shape=jax.ShapeDtypeStruct((X * HALF, H), BF16),
        in_specs=[VMEM],
        out_specs=VMEM,
        compiler_params=pltpu.CompilerParams(vmem_limit_bytes=16 * 1024 * 1024),
        name="halve",
    )(received)


def finish_kernel(g_ref, w1s_ref, w1n_ref, w2s_ref, w2n_ref, w3_ref, sems):
    copies = [
        pltpu.make_async_copy(g_ref.at[pl.ds(0, H), :], w2s_ref, sems.at[0]),
        pltpu.make_async_copy(g_ref.at[pl.ds(H, H), :], w2n_ref, sems.at[1]),
    ]
    for copy in copies:
        copy.start()
    first = g_ref[pl.ds(AT_FIRST, 32), :]
    w1s_ref[...] = first[:COLS]
    w1n_ref[...] = first[16 : 16 + COLS]
    w3_ref[...] = g_ref[pl.ds(AT_THIRD, C), :]
    for copy in copies:
        copy.wait()


def finish(gradients):
    shapes = [(COLS, H), (COLS, H), (H, H), (H, H), (C, H)]
    anywhere = pl.BlockSpec(memory_space=pl.ANY)
    return pl.pallas_call(
        finish_kernel,
        out_shape=tuple(jax.ShapeDtypeStruct(shape, F32) for shape in shapes),
        in_specs=[VMEM],
        out_specs=(VMEM, VMEM, anywhere, anywhere, VMEM),
        scratch_shapes=[pltpu.SemaphoreType.DMA((2,))],
        compiler_params=pltpu.CompilerParams(vmem_limit_bytes=16 * 1024 * 1024),
        name="finish",
    )(gradients)


def exchange(rows, axis, parts):
    received = lax.all_to_all(rows.reshape(parts, -1, rows.shape[1]), axis, 0, 0)
    return received.reshape(rows.shape)


def local(features, nbr_ids, nbr_counts, self_ids, seed_counts, labels, w1_self, w1_nbr, w2_self, w2_nbr, w3):
    packed = gather(self_ids, nbr_ids.T, nbr_counts, features, w1_self, w1_nbr)
    shares, left = project(exchange(packed, "y", Y))
    pre_one = exchange(spread(exchange(shares, "z", Z)), "z", Z)
    place = lax.axis_index("y").astype(jnp.int32)[None]
    back = seeds(place, pre_one, left, seed_counts, labels, w2_self, w2_nbr, w3.T)
    grads = weights(exchange(back, "y", Y), labels, w2_self, w2_nbr, w3.T)
    grads = exchange(halve(exchange(grads, "core", CORE)), "x", X)
    summed = jnp.sum(grads.reshape(X, HALF, H).astype(F32), axis=0)
    whole = lax.all_gather(summed, "core", axis=0, tiled=True)
    grad_w1s, grad_w1n, grad_w2s, grad_w2n, grad_w3 = finish(whole)
    return grad_w1s, grad_w1n, grad_w2s, grad_w2n, grad_w3.T


def solution(mesh):
    split = Mesh(mesh.devices.reshape(Z, Y, X, CORE), ("z", "y", "x", "core"))
    feat, batch = P(("z", "y"), None), P(("x", "core"))
    in_specs = (feat, P(("x", "core"), None), batch, batch, batch, batch, feat, feat, P(), P(), P())
    out_specs = (feat, feat, P(), P(), P())
    return jax.shard_map(local, mesh=split, in_specs=in_specs, out_specs=out_specs, check_vma=False)
```

```python
import jax
import jax.numpy as jnp
from jax import lax
from jax.experimental import pallas as pl
from jax.experimental.pallas import tpu as pltpu
from jax.sharding import Mesh, PartitionSpec as P

NODES = 65536
COLS = 11
H = 256
C = 172
FAN1 = 15
FAN2 = 10
IDS = 1 + FAN1
KEEP = 1 + FAN2
SEEDS_B = 192
ROWS_B = SEEDS_B * KEEP
Z, Y, X, CORE = 12, 8, 4, 2
BATCH = X * CORE
LOSS_SCALE = 1.0 / (SEEDS_B * BATCH)
SEEDS_Y = SEEDS_B // Y
ROWS_Y = SEEDS_Y * KEEP
GROUPS = 3
PACKED = ROWS_Y // GROUPS
SLOTS = 8
SLOT_ROWS = NODES // SLOTS
CHUNK = 64
CHUNKS = ROWS_B // CHUNK
AHEAD = 4
WIDE = 24
SEND = 144
SHARE = 24
ROWS_Z = Z * SHARE
BACK = 32 + 2 * SEEDS_Y
AT_FIRST = 2 * H
AT_THIRD = AT_FIRST + 32
HALF = 368
PIECES = 2
BF16 = jnp.bfloat16
F32 = jnp.float32
VMEM = pl.BlockSpec(memory_space=pltpu.VMEM)
SMEM = pl.BlockSpec(memory_space=pltpu.SMEM)
HBM = pl.BlockSpec(memory_space=pltpu.HBM)


def gather_kernel(
    self_in, nbr_in, counts_in, x_in, w1s_in, w1n_in, o_ref,
    self_ref, nbr_ref, counts_ref, x_ref, w1s_ref, w1n_ref, small_sems, x_sems,
    table, own_ref, agg_ref, ids, near, sems,
):
    lane = lax.broadcasted_iota(jnp.int32, (1, 128), 1)
    small = [(self_in, self_ref), (nbr_in, nbr_ref), (counts_in, counts_ref), (w1s_in, w1s_ref), (w1n_in, w1n_ref)]
    small = [pltpu.make_async_copy(source, target, small_sems.at[i]) for i, (source, target) in enumerate(small)]
    for copy in small:
        copy.start()
    pieces = []
    for piece in range(PIECES):
        pieces.append([])
        for slot in range(SLOTS):
            place = pl.ds(slot * SLOT_ROWS + piece * (SLOT_ROWS // PIECES), SLOT_ROWS // PIECES)
            pieces[piece].append(pltpu.make_async_copy(x_in.at[:, place], x_ref.at[:, place], x_sems.at[piece, slot]))
            pieces[piece][slot].start()
    def fetch(chunk, slot):
        return pltpu.make_async_copy(ids.at[chunk], near[slot], sems.at[slot])

    def tabulate(piece):
        for copy in pieces[piece]:
            copy.wait()

        @pl.loop(0, SLOT_ROWS // PIECES // 128, unroll=8)
        def _(step):
            block = step + piece * (SLOT_ROWS // PIECES // 128)
            stacked = []
            for slot in range(SLOTS):
                start = pl.multiple_of(slot * SLOT_ROWS + block * 128, 128)
                stacked += [x_ref[:, pl.ds(start, 128)].astype(F32), jnp.ones((1, 128), F32), jnp.zeros((4, 128), F32)]
            turned = jnp.concatenate(stacked, 0).astype(BF16).T.astype(F32)
            for slot in range(SLOTS):
                start = pl.multiple_of(slot * SLOT_ROWS + block * 128, 128)
                table[pl.ds(start, 128), :] = jnp.where(lane // 16 == slot, turned, 0.0)

    tabulate(0)
    for copy in small:
        copy.wait()
    counts = counts_ref[...][None, :]
    valid = lax.broadcasted_iota(jnp.int32, (FAN1, ROWS_B), 0) < counts
    both = jnp.concatenate([jnp.where(valid, nbr_ref[...], NODES), self_ref[...][None, :]], 0)
    both = jnp.concatenate([both, jnp.zeros((IDS, CHUNK), jnp.int32)], 1)
    for tile in range(-(-ROWS_B // 128)):
        low, high = both[:8, tile * 128 :][:, :128], both[8:, tile * 128 :][:, :128]
        ids[2 * tile] = jnp.where(lane < CHUNK, low, pltpu.roll(high, CHUNK, 1))
        if 2 * tile + 1 < CHUNKS:
            ids[2 * tile + 1] = jnp.where(lane < CHUNK, pltpu.roll(low, CHUNK, 1), high)
    for slot in range(AHEAD):
        fetch(slot, slot).start()
    for piece in range(1, PIECES):
        tabulate(piece)
    table[pl.ds(NODES, 8), :] = jnp.zeros((8, 128), F32)

    def take(chunk, slot):
        fetch(chunk, slot).wait()
        first = chunk * CHUNK
        for i in range(CHUNK):
            rows = [table[pl.ds(near[slot][j % 8, j // 8 * CHUNK + i], 1), :] for j in range(IDS)]
            own_ref[pl.ds(first + i, 1), :] = rows.pop()
            while len(rows) > 1:
                rows = [sum(rows[a : a + 2]) for a in range(0, len(rows), 2)]
            agg_ref[pl.ds(first + i, 1), :] = rows[0]

    @pl.loop(0, CHUNKS // AHEAD)
    def _(turn):
        for slot in range(AHEAD):
            chunk = turn * AHEAD + slot
            take(chunk, slot)

            @pl.when(chunk + AHEAD < CHUNKS)
            def _():
                fetch(chunk + AHEAD, slot).start()

    for slot in range(CHUNKS % AHEAD):
        take(CHUNKS // AHEAD * AHEAD + slot, slot)

    def halves(low, high, width):
        mask = lane % (2 * width) < width
        if high is None:
            return jnp.where(mask, low + pltpu.roll(low, 128 - width, 1), 0.0)
        moved = jnp.where(mask, pltpu.roll(low, 128 - width, 1), pltpu.roll(high, width, 1))
        return jnp.where(mask, low, high) + moved

    w1 = jnp.concatenate([w1s_ref[...].astype(F32), w1n_ref[...].astype(F32), jnp.zeros((WIDE - 2 * COLS, H), F32)], 0)
    w1 = [w1[:, :128], w1[:, 128:], jnp.zeros((SEND - PACKED - 2 * WIDE, 128), F32)]
    row = lax.broadcasted_iota(jnp.int32, (128, 128), 0)
    column = lax.broadcasted_iota(jnp.int32, (128, 128), 1)
    counter = jnp.where((row % 16 == COLS) & (row // 16 == column // 16), 1.0, 0.0).astype(BF16)

    @pl.loop(0, Y, unroll=2)
    def _(block):
        message = []
        for step in range(PACKED // 8):
            v = []
            for group in range(GROUPS):
                place = pl.ds(pl.multiple_of(block * ROWS_Y + group * PACKED + step * 8, 8), 8)
                v += [own_ref[place, :], agg_ref[place, :]]
            v = [halves(v[q], v[q + 4] if q < 2 else None, 64) for q in range(4)]
            v = [halves(v[q], v[q + 2], 32) for q in range(2)]
            message.append(halves(v[0], v[1], 16))
        packed = jnp.concatenate(message, 0)
        counted = jnp.dot(packed.astype(BF16), counter, preferred_element_type=F32)
        packed = jnp.where((lane < GROUPS * 32) & (lane % 16 < COLS), packed / counted, 0.0)
        message = jnp.concatenate([packed] + w1, 0).astype(BF16)
        o_ref[pl.ds(pl.multiple_of(block * SEND, 16), SEND), :] = message


def gather(self_ids, nbr_ids, counts, features, w1_self, w1_nbr):
    return pl.pallas_call(
        gather_kernel,
        out_shape=jax.ShapeDtypeStruct((Y * SEND, 128), BF16),
        in_specs=[HBM] * 6,
        out_specs=VMEM,
        scratch_shapes=[
            pltpu.VMEM((ROWS_B,), jnp.int32),
            pltpu.VMEM((FAN1, ROWS_B), jnp.int32),
            pltpu.VMEM((ROWS_B,), jnp.int32),
            pltpu.VMEM((COLS, NODES), BF16),
            pltpu.VMEM((COLS, H), BF16),
            pltpu.VMEM((COLS, H), BF16),
            pltpu.SemaphoreType.DMA((5,)),
            pltpu.SemaphoreType.DMA((PIECES, SLOTS)),
            pltpu.VMEM((NODES + 8, 128), F32),
            pltpu.VMEM((ROWS_B, 128), F32),
            pltpu.VMEM((ROWS_B, 128), F32),
            pltpu.VMEM((CHUNKS, 8, 128), jnp.int32),
            [pltpu.SMEM((8, 128), jnp.int32)] * AHEAD,
            pltpu.SemaphoreType.DMA((AHEAD,)),
        ],
        compiler_params=pltpu.CompilerParams(vmem_limit_bytes=63 * 1024 * 1024),
        name="gather",
    )(self_ids, nbr_ids, counts, features, w1_self, w1_nbr)


def project_kernel(r_ref, o_ref, left_ref):
    lane = lax.broadcasted_iota(jnp.int32, (1, 128), 1)
    blocks = [r_ref[pl.ds(y * SEND, SEND), :].astype(F32) for y in range(Y)]
    right = []
    gap = jnp.zeros((16 - COLS, H), F32)
    for block in blocks:
        rows = jnp.concatenate([block[PACKED + half * WIDE :][:WIDE] for half in range(2)], 1)
        right += [rows[:COLS], gap, rows[COLS : 2 * COLS], gap]
    right = jnp.concatenate(right, 0).astype(BF16)
    left = []
    for group in range(GROUPS):
        halves = []
        for half in range(2):
            mixed = jnp.zeros((PACKED, 128), F32)
            for j in range(4):
                one = blocks[half * 4 + j][:PACKED]
                shift = (j - group) * 32 % 128
                one = pltpu.roll(one, shift, 1) if shift else one
                mixed = jnp.where(lane // 32 == j, one, mixed)
            halves.append(mixed)
        left.append(jnp.concatenate(halves, 1))
    left = jnp.concatenate(left, 0).astype(BF16)
    left_ref[...] = left
    total = jnp.dot(left, right, preferred_element_type=F32)
    o_ref[...] = jnp.concatenate([total, jnp.zeros((ROWS_Z - ROWS_Y, H), F32)], 0).astype(BF16)


def project(received):
    return pl.pallas_call(
        project_kernel,
        out_shape=(jax.ShapeDtypeStruct((ROWS_Z, H), BF16), jax.ShapeDtypeStruct((ROWS_Y, Y * 32), BF16)),
        in_specs=[VMEM],
        out_specs=(VMEM, VMEM),
        compiler_params=pltpu.CompilerParams(vmem_limit_bytes=32 * 1024 * 1024),
        name="project",
    )(received)


def spread_kernel(s_ref, o_ref):
    total = jnp.zeros((SHARE, H), F32)
    for pair in range(Z // 2):
        both = s_ref[pl.ds(pair * 2 * SHARE, 2 * SHARE), :].astype(F32)
        total = total + (both[:SHARE] + both[SHARE:])
    twice = jnp.concatenate([total, total], 0).astype(BF16)
    for pair in range(Z // 2):
        o_ref[pl.ds(pair * 2 * SHARE, 2 * SHARE), :] = twice


def spread(shares):
    return pl.pallas_call(
        spread_kernel,
        out_shape=jax.ShapeDtypeStruct((ROWS_Z, H), BF16),
        in_specs=[VMEM],
        out_specs=VMEM,
        compiler_params=pltpu.CompilerParams(vmem_limit_bytes=16 * 1024 * 1024),
        name="spread",
    )(shares)


def sigmoid(value):
    return 1.0 / (1.0 + jnp.exp(-value))


def outer_cols(left, right):
    return lax.dot_general(left, right, (((1,), (1,)), ((), ())), preferred_element_type=F32)


def inner_rows(left, right):
    return lax.dot_general(left, right, (((0,), (0,)), ((), ())), preferred_element_type=F32)


def top(head, mean_two, labels, w2_self, w2_nbr, w3):
    pre_two = jnp.dot(head, w2_self, preferred_element_type=F32) + jnp.dot(mean_two, w2_nbr, preferred_element_type=F32)
    sig_two = sigmoid(pre_two)
    act_two = (pre_two * sig_two).astype(BF16)
    slope_two = sig_two * (1.0 + pre_two * (1.0 - sig_two))
    logits = outer_cols(act_two, w3)
    expsum = jnp.exp(logits - jnp.max(logits, axis=1, keepdims=True))
    probability = expsum / jnp.sum(expsum, axis=1, keepdims=True)
    onehot = (lax.broadcasted_iota(jnp.int32, logits.shape, 1) == labels).astype(F32)
    grad_three = ((probability - onehot) * LOSS_SCALE).astype(BF16)
    grad_two = (jnp.dot(grad_three, w3, preferred_element_type=F32) * slope_two).astype(BF16)
    return act_two, grad_three, grad_two


def as_column(ref, first, rows):
    row = lax.broadcasted_iota(jnp.int32, (rows, SEEDS_B), 0) + first
    column = lax.broadcasted_iota(jnp.int32, (rows, SEEDS_B), 1)
    spread_out = jnp.where(row == column, ref[...][None, :], 0).astype(F32)
    return jnp.sum(spread_out, axis=1, keepdims=True).astype(jnp.int32)


def seeds_kernel(place_ref, z_ref, left_ref, counts_ref, labels_ref, w2s_ref, w2n_ref, w3_ref, o_ref, stage):
    first = place_ref[0] * SEEDS_Y
    counts = as_column(counts_ref, first, SEEDS_Y)
    scale = counts.astype(F32)
    pre_one = z_ref[...].astype(F32)[:ROWS_Y]
    sig_one = sigmoid(pre_one)
    act_one = (pre_one * sig_one).astype(BF16)
    slope_one = sig_one * (1.0 + pre_one * (1.0 - sig_one))
    behind = lax.broadcasted_iota(jnp.int32, (SEEDS_Y, ROWS_Y), 1) - KEEP * lax.broadcasted_iota(jnp.int32, (SEEDS_Y, ROWS_Y), 0)

    def choose(mask):
        return jnp.where(mask, 1.0, 0.0).astype(BF16)

    kept = choose((behind > 0) & (behind <= counts))
    belongs = choose((behind >= 0) & (behind < KEEP))
    is_head = choose(behind == 0)
    head = jnp.dot(is_head, act_one, preferred_element_type=F32).astype(BF16)
    mean_two = (jnp.dot(kept, act_one, preferred_element_type=F32) / scale).astype(BF16)
    _, _, grad_two = top(head, mean_two, as_column(labels_ref, first, SEEDS_Y), w2s_ref[...], w2n_ref[...], w3_ref[...])
    ones = jnp.ones((SEEDS_Y, H), BF16)
    grad_rows = inner_rows(belongs, grad_two).astype(BF16)
    scale_rows = inner_rows(belongs, (ones * scale).astype(BF16))
    grad_mean = outer_cols(grad_rows, w2n_ref[...]) / scale_rows
    grad = jnp.where(inner_rows(kept, ones) > 0.5, grad_mean, 0.0)
    grad = jnp.where(inner_rows(is_head, ones) > 0.5, outer_cols(grad_rows, w2s_ref[...]), grad)
    grad_one = inner_rows(left_ref[...], (grad * slope_one).astype(BF16))
    for y in range(Y):
        stage[pl.ds(y * BACK, 32), :] = grad_one[y * 32 :][:32]
        stage[pl.ds(y * BACK + 32, SEEDS_Y), :] = head.astype(F32)
        stage[pl.ds(y * BACK + 32 + SEEDS_Y, SEEDS_Y), :] = mean_two.astype(F32)
    o_ref[...] = stage[...].astype(BF16)


def seeds(place, pre_one, left, counts, labels, w2_self, w2_nbr, w3):
    return pl.pallas_call(
        seeds_kernel,
        out_shape=jax.ShapeDtypeStruct((Y * BACK, H), BF16),
        in_specs=[SMEM] + [VMEM] * 7,
        out_specs=VMEM,
        scratch_shapes=[pltpu.VMEM((Y * BACK, H), F32)],
        compiler_params=pltpu.CompilerParams(vmem_limit_bytes=32 * 1024 * 1024),
        name="seeds",
    )(place, pre_one, left, counts, labels, w2_self, w2_nbr, w3)


def weights_kernel(r_ref, labels_ref, w2s_ref, w2n_ref, w3_ref, o_ref):
    rows = r_ref[...].astype(F32)
    grad_one = jnp.zeros((32, H), F32)
    head, mean_two = [], []
    for y in range(Y):
        grad_one = grad_one + rows[y * BACK :][:32]
        head.append(rows[y * BACK + 32 :][:SEEDS_Y])
        mean_two.append(rows[y * BACK + 32 + SEEDS_Y :][:SEEDS_Y])
    head = jnp.concatenate(head, 0).astype(BF16)
    mean_two = jnp.concatenate(mean_two, 0).astype(BF16)
    act_two, grad_three, grad_two = top(head, mean_two, as_column(labels_ref, 0, SEEDS_B), w2s_ref[...], w2n_ref[...], w3_ref[...])
    o_ref[pl.ds(0, H), :] = inner_rows(head, grad_two)
    o_ref[pl.ds(H, H), :] = inner_rows(mean_two, grad_two)
    o_ref[pl.ds(AT_FIRST, 32), :] = grad_one
    o_ref[pl.ds(AT_THIRD, C), :] = inner_rows(grad_three, act_two)
    rest = 2 * HALF - AT_THIRD - C
    o_ref[pl.ds(AT_THIRD + C, rest), :] = jnp.zeros((rest, H), F32)


def weights(received, labels, w2_self, w2_nbr, w3):
    return pl.pallas_call(
        weights_kernel,
        out_shape=jax.ShapeDtypeStruct((2 * HALF, H), F32),
        in_specs=[VMEM] * 5,
        out_specs=VMEM,
        compiler_params=pltpu.CompilerParams(vmem_limit_bytes=32 * 1024 * 1024),
        name="weights",
    )(received, labels, w2_self, w2_nbr, w3)


def halve_kernel(g_ref, o_ref):
    total = (g_ref[pl.ds(0, HALF), :] + g_ref[pl.ds(HALF, HALF), :]).astype(BF16)
    for x in range(X):
        o_ref[pl.ds(x * HALF, HALF), :] = total


def halve(received):
    return pl.pallas_call(
        halve_kernel,
        out_shape=jax.ShapeDtypeStruct((X * HALF, H), BF16),
        in_specs=[VMEM],
        out_specs=VMEM,
        compiler_params=pltpu.CompilerParams(vmem_limit_bytes=16 * 1024 * 1024),
        name="halve",
    )(received)


def finish_kernel(g_ref, w1s_ref, w1n_ref, w2s_ref, w2n_ref, w3_ref, sems):
    copies = [
        pltpu.make_async_copy(g_ref.at[pl.ds(0, H), :], w2s_ref, sems.at[0]),
        pltpu.make_async_copy(g_ref.at[pl.ds(H, H), :], w2n_ref, sems.at[1]),
    ]
    for copy in copies:
        copy.start()
    first = g_ref[pl.ds(AT_FIRST, 32), :]
    w1s_ref[...] = first[:COLS]
    w1n_ref[...] = first[16 : 16 + COLS]
    w3_ref[...] = g_ref[pl.ds(AT_THIRD, C), :]
    for copy in copies:
        copy.wait()


def finish(gradients):
    shapes = [(COLS, H), (COLS, H), (H, H), (H, H), (C, H)]
    anywhere = pl.BlockSpec(memory_space=pl.ANY)
    return pl.pallas_call(
        finish_kernel,
        out_shape=tuple(jax.ShapeDtypeStruct(shape, F32) for shape in shapes),
        in_specs=[VMEM],
        out_specs=(VMEM, VMEM, anywhere, anywhere, VMEM),
        scratch_shapes=[pltpu.SemaphoreType.DMA((2,))],
        compiler_params=pltpu.CompilerParams(vmem_limit_bytes=16 * 1024 * 1024),
        name="finish",
    )(gradients)


def exchange(rows, axis, parts):
    received = lax.all_to_all(rows.reshape(parts, -1, rows.shape[1]), axis, 0, 0)
    return received.reshape(rows.shape)


def local(features, nbr_ids, nbr_counts, self_ids, seed_counts, labels, w1_self, w1_nbr, w2_self, w2_nbr, w3):
    packed = gather(self_ids, nbr_ids.T, nbr_counts, features, w1_self, w1_nbr)
    shares, left = project(exchange(packed, "y", Y))
    pre_one = exchange(spread(exchange(shares, "z", Z)), "z", Z)
    place = lax.axis_index("y").astype(jnp.int32)[None]
    back = seeds(place, pre_one, left, seed_counts, labels, w2_self, w2_nbr, w3.T)
    grads = weights(exchange(back, "y", Y), labels, w2_self, w2_nbr, w3.T)
    grads = exchange(halve(exchange(grads, "core", CORE)), "x", X)
    summed = jnp.sum(grads.reshape(X, HALF, H).astype(F32), axis=0)
    whole = lax.all_gather(summed, "core", axis=0, tiled=True)
    grad_w1s, grad_w1n, grad_w2s, grad_w2n, grad_w3 = finish(whole)
    return grad_w1s, grad_w1n, grad_w2s, grad_w2n, grad_w3.T


def solution(mesh):
    split = Mesh(mesh.devices.reshape(Z, Y, X, CORE), ("z", "y", "x", "core"))
    feat, batch = P(("z", "y"), None), P(("x", "core"))
    in_specs = (feat, P(("x", "core"), None), batch, batch, batch, batch, feat, feat, P(), P(), P())
    out_specs = (feat, feat, P(), P(), P())
    return jax.shard_map(local, mesh=split, in_specs=in_specs, out_specs=out_specs, check_vma=False)
```

```python
import jax
import jax.numpy as jnp
from jax import lax
from jax.experimental import pallas as pl
from jax.experimental.pallas import tpu as pltpu
from jax.sharding import Mesh, PartitionSpec as P

NODES = 65536
COLS = 11
H = 256
C = 172
FAN1 = 15
FAN2 = 10
IDS = 1 + FAN1
KEEP = 1 + FAN2
SEEDS_B = 192
ROWS_B = SEEDS_B * KEEP
Z, Y, X, CORE = 12, 8, 4, 2
BATCH = X * CORE
LOSS_SCALE = 1.0 / (SEEDS_B * BATCH)
SEEDS_Y = SEEDS_B // Y
ROWS_Y = SEEDS_Y * KEEP
GROUPS = 3
PACKED = ROWS_Y // GROUPS
SLOTS = 8
SLOT_ROWS = NODES // SLOTS
CHUNK = 64
CHUNKS = ROWS_B // CHUNK
AHEAD = 4
WIDE = 24
SEND = 144
SHARE = 24
ROWS_Z = Z * SHARE
BACK = 32 + 2 * SEEDS_Y
AT_FIRST = 2 * H
AT_THIRD = AT_FIRST + 32
HALF = 368
PIECES = 2
BF16 = jnp.bfloat16
F32 = jnp.float32
VMEM = pl.BlockSpec(memory_space=pltpu.VMEM)
HBM = pl.BlockSpec(memory_space=pltpu.HBM)


def gather_kernel(
    self_in, nbr_in, counts_in, x_in, w1s_in, w1n_in, o_ref,
    self_ref, nbr_ref, counts_ref, x_ref, w1s_ref, w1n_ref, small_sems, x_sems,
    table, own_ref, agg_ref, ids, near, sems,
):
    lane = lax.broadcasted_iota(jnp.int32, (1, 128), 1)
    small = [(self_in, self_ref), (nbr_in, nbr_ref), (counts_in, counts_ref), (w1s_in, w1s_ref), (w1n_in, w1n_ref)]
    small = [pltpu.make_async_copy(source, target, small_sems.at[i]) for i, (source, target) in enumerate(small)]
    for copy in small:
        copy.start()
    pieces = []
    for piece in range(PIECES):
        pieces.append([])
        for slot in range(SLOTS):
            place = pl.ds(slot * SLOT_ROWS + piece * (SLOT_ROWS // PIECES), SLOT_ROWS // PIECES)
            pieces[piece].append(pltpu.make_async_copy(x_in.at[:, place], x_ref.at[:, place], x_sems.at[piece, slot]))
            pieces[piece][slot].start()
    def fetch(chunk, slot):
        return pltpu.make_async_copy(ids.at[chunk], near[slot], sems.at[slot])

    def tabulate(piece):
        for copy in pieces[piece]:
            copy.wait()

        @pl.loop(0, SLOT_ROWS // PIECES // 128, unroll=8)
        def _(step):
            block = step + piece * (SLOT_ROWS // PIECES // 128)
            stacked = []
            for slot in range(SLOTS):
                start = pl.multiple_of(slot * SLOT_ROWS + block * 128, 128)
                stacked += [x_ref[:, pl.ds(start, 128)].astype(F32), jnp.ones((1, 128), F32), jnp.zeros((4, 128), F32)]
            turned = jnp.concatenate(stacked, 0).astype(BF16).T.astype(F32)
            for slot in range(SLOTS):
                start = pl.multiple_of(slot * SLOT_ROWS + block * 128, 128)
                table[pl.ds(start, 128), :] = jnp.where(lane // 16 == slot, turned, 0.0)

    tabulate(0)
    for copy in small:
        copy.wait()
    counts = counts_ref[...][None, :]
    valid = lax.broadcasted_iota(jnp.int32, (FAN1, ROWS_B), 0) < counts
    both = jnp.concatenate([jnp.where(valid, nbr_ref[...], NODES), self_ref[...][None, :]], 0)
    both = jnp.concatenate([both, jnp.zeros((IDS, CHUNK), jnp.int32)], 1)
    for tile in range(-(-ROWS_B // 128)):
        low, high = both[:8, tile * 128 :][:, :128], both[8:, tile * 128 :][:, :128]
        ids[2 * tile] = jnp.where(lane < CHUNK, low, pltpu.roll(high, CHUNK, 1))
        if 2 * tile + 1 < CHUNKS:
            ids[2 * tile + 1] = jnp.where(lane < CHUNK, pltpu.roll(low, CHUNK, 1), high)
    for slot in range(AHEAD):
        fetch(slot, slot).start()
    for piece in range(1, PIECES):
        tabulate(piece)
    table[pl.ds(NODES, 8), :] = jnp.zeros((8, 128), F32)

    def take(chunk, slot):
        fetch(chunk, slot).wait()
        first = chunk * CHUNK
        for i in range(CHUNK):
            rows = [table[pl.ds(near[slot][j % 8, j // 8 * CHUNK + i], 1), :] for j in range(IDS)]
            own_ref[pl.ds(first + i, 1), :] = rows.pop()
            while len(rows) > 1:
                rows = [sum(rows[a : a + 2]) for a in range(0, len(rows), 2)]
            agg_ref[pl.ds(first + i, 1), :] = rows[0]

    @pl.loop(0, CHUNKS // AHEAD)
    def _(turn):
        for slot in range(AHEAD):
            chunk = turn * AHEAD + slot
            take(chunk, slot)

            @pl.when(chunk + AHEAD < CHUNKS)
            def _():
                fetch(chunk + AHEAD, slot).start()

    for slot in range(CHUNKS % AHEAD):
        take(CHUNKS // AHEAD * AHEAD + slot, slot)

    def halves(low, high, width):
        mask = lane % (2 * width) < width
        if high is None:
            return jnp.where(mask, low + pltpu.roll(low, 128 - width, 1), 0.0)
        moved = jnp.where(mask, pltpu.roll(low, 128 - width, 1), pltpu.roll(high, width, 1))
        return jnp.where(mask, low, high) + moved

    w1 = jnp.concatenate([w1s_ref[...].astype(F32), w1n_ref[...].astype(F32), jnp.zeros((WIDE - 2 * COLS, H), F32)], 0)
    w1 = [w1[:, :128], w1[:, 128:], jnp.zeros((SEND - PACKED - 2 * WIDE, 128), F32)]
    row = lax.broadcasted_iota(jnp.int32, (128, 128), 0)
    column = lax.broadcasted_iota(jnp.int32, (128, 128), 1)
    counter = jnp.where((row % 16 == COLS) & (row // 16 == column // 16), 1.0, 0.0).astype(BF16)

    @pl.loop(0, Y, unroll=2)
    def _(block):
        message = []
        for step in range(PACKED // 8):
            v = []
            for group in range(GROUPS):
                place = pl.ds(pl.multiple_of(block * ROWS_Y + group * PACKED + step * 8, 8), 8)
                v += [own_ref[place, :], agg_ref[place, :]]
            v = [halves(v[q], v[q + 4] if q < 2 else None, 64) for q in range(4)]
            v = [halves(v[q], v[q + 2], 32) for q in range(2)]
            message.append(halves(v[0], v[1], 16))
        packed = jnp.concatenate(message, 0)
        counted = jnp.dot(packed.astype(BF16), counter, preferred_element_type=F32)
        packed = jnp.where((lane < GROUPS * 32) & (lane % 16 < COLS), packed / counted, 0.0)
        message = jnp.concatenate([packed] + w1, 0).astype(BF16)
        o_ref[pl.ds(pl.multiple_of(block * SEND, 16), SEND), :] = message


def gather(self_ids, nbr_ids, counts, features, w1_self, w1_nbr):
    return pl.pallas_call(
        gather_kernel,
        out_shape=jax.ShapeDtypeStruct((Y * SEND, 128), BF16),
        in_specs=[HBM] * 6,
        out_specs=VMEM,
        scratch_shapes=[
            pltpu.VMEM((ROWS_B,), jnp.int32),
            pltpu.VMEM((FAN1, ROWS_B), jnp.int32),
            pltpu.VMEM((ROWS_B,), jnp.int32),
            pltpu.VMEM((COLS, NODES), BF16),
            pltpu.VMEM((COLS, H), BF16),
            pltpu.VMEM((COLS, H), BF16),
            pltpu.SemaphoreType.DMA((5,)),
            pltpu.SemaphoreType.DMA((PIECES, SLOTS)),
            pltpu.VMEM((NODES + 8, 128), F32),
            pltpu.VMEM((ROWS_B, 128), F32),
            pltpu.VMEM((ROWS_B, 128), F32),
            pltpu.VMEM((CHUNKS, 8, 128), jnp.int32),
            [pltpu.SMEM((8, 128), jnp.int32)] * AHEAD,
            pltpu.SemaphoreType.DMA((AHEAD,)),
        ],
        compiler_params=pltpu.CompilerParams(vmem_limit_bytes=63 * 1024 * 1024),
        name="gather",
    )(self_ids, nbr_ids, counts, features, w1_self, w1_nbr)


def project_kernel(r_ref, o_ref, left_ref):
    lane = lax.broadcasted_iota(jnp.int32, (1, 128), 1)
    blocks = [r_ref[pl.ds(y * SEND, SEND), :].astype(F32) for y in range(Y)]
    right = []
    gap = jnp.zeros((16 - COLS, H), F32)
    for block in blocks:
        rows = jnp.concatenate([block[PACKED + half * WIDE :][:WIDE] for half in range(2)], 1)
        right += [rows[:COLS], gap, rows[COLS : 2 * COLS], gap]
    right = jnp.concatenate(right, 0).astype(BF16)
    left = []
    for group in range(GROUPS):
        halves = []
        for half in range(2):
            mixed = jnp.zeros((PACKED, 128), F32)
            for j in range(4):
                one = blocks[half * 4 + j][:PACKED]
                shift = (j - group) * 32 % 128
                one = pltpu.roll(one, shift, 1) if shift else one
                mixed = jnp.where(lane // 32 == j, one, mixed)
            halves.append(mixed)
        left.append(jnp.concatenate(halves, 1))
    left = jnp.concatenate(left, 0).astype(BF16)
    left_ref[...] = left
    total = jnp.dot(left, right, preferred_element_type=F32)
    o_ref[...] = jnp.concatenate([total, jnp.zeros((ROWS_Z - ROWS_Y, H), F32)], 0).astype(BF16)


def project(received):
    return pl.pallas_call(
        project_kernel,
        out_shape=(jax.ShapeDtypeStruct((ROWS_Z, H), BF16), jax.ShapeDtypeStruct((ROWS_Y, Y * 32), BF16)),
        in_specs=[VMEM],
        out_specs=(VMEM, VMEM),
        compiler_params=pltpu.CompilerParams(vmem_limit_bytes=32 * 1024 * 1024),
        name="project",
    )(received)


def spread_kernel(s_ref, o_ref):
    total = jnp.zeros((SHARE, H), F32)
    for pair in range(Z // 2):
        both = s_ref[pl.ds(pair * 2 * SHARE, 2 * SHARE), :].astype(F32)
        total = total + (both[:SHARE] + both[SHARE:])
    twice = jnp.concatenate([total, total], 0).astype(BF16)
    for pair in range(Z // 2):
        o_ref[pl.ds(pair * 2 * SHARE, 2 * SHARE), :] = twice


def spread(shares):
    return pl.pallas_call(
        spread_kernel,
        out_shape=jax.ShapeDtypeStruct((ROWS_Z, H), BF16),
        in_specs=[VMEM],
        out_specs=VMEM,
        compiler_params=pltpu.CompilerParams(vmem_limit_bytes=16 * 1024 * 1024),
        name="spread",
    )(shares)


def sigmoid(value):
    return 1.0 / (1.0 + jnp.exp(-value))


def outer_cols(left, right):
    return lax.dot_general(left, right, (((1,), (1,)), ((), ())), preferred_element_type=F32)


def inner_rows(left, right):
    return lax.dot_general(left, right, (((0,), (0,)), ((), ())), preferred_element_type=F32)


def top(head, mean_two, labels, w2_self, w2_nbr, w3):
    pre_two = jnp.dot(head, w2_self, preferred_element_type=F32) + jnp.dot(mean_two, w2_nbr, preferred_element_type=F32)
    sig_two = sigmoid(pre_two)
    act_two = (pre_two * sig_two).astype(BF16)
    slope_two = sig_two * (1.0 + pre_two * (1.0 - sig_two))
    logits = outer_cols(act_two, w3)
    expsum = jnp.exp(logits - jnp.max(logits, axis=1, keepdims=True))
    probability = expsum / jnp.sum(expsum, axis=1, keepdims=True)
    onehot = (lax.broadcasted_iota(jnp.int32, logits.shape, 1) == labels).astype(F32)
    grad_three = ((probability - onehot) * LOSS_SCALE).astype(BF16)
    grad_two = (jnp.dot(grad_three, w3, preferred_element_type=F32) * slope_two).astype(BF16)
    return act_two, grad_three, grad_two


def as_column(ref, first, rows):
    row = lax.broadcasted_iota(jnp.int32, (rows, SEEDS_B), 0) + first
    column = lax.broadcasted_iota(jnp.int32, (rows, SEEDS_B), 1)
    spread_out = jnp.where(row == column, ref[...][None, :], 0).astype(F32)
    return jnp.sum(spread_out, axis=1, keepdims=True).astype(jnp.int32)


def seeds_kernel(z_ref, left_ref, counts_ref, labels_ref, w2s_ref, w2n_ref, w3_ref, o_ref, stage):
    first = lax.axis_index("y") * SEEDS_Y
    counts = as_column(counts_ref, first, SEEDS_Y)
    scale = counts.astype(F32)
    pre_one = z_ref[...].astype(F32)[:ROWS_Y]
    sig_one = sigmoid(pre_one)
    act_one = (pre_one * sig_one).astype(BF16)
    slope_one = sig_one * (1.0 + pre_one * (1.0 - sig_one))
    behind = lax.broadcasted_iota(jnp.int32, (SEEDS_Y, ROWS_Y), 1) - KEEP * lax.broadcasted_iota(jnp.int32, (SEEDS_Y, ROWS_Y), 0)

    def choose(mask):
        return jnp.where(mask, 1.0, 0.0).astype(BF16)

    kept = choose((behind > 0) & (behind <= counts))
    belongs = choose((behind >= 0) & (behind < KEEP))
    is_head = choose(behind == 0)
    head = jnp.dot(is_head, act_one, preferred_element_type=F32).astype(BF16)
    mean_two = (jnp.dot(kept, act_one, preferred_element_type=F32) / scale).astype(BF16)
    _, _, grad_two = top(head, mean_two, as_column(labels_ref, first, SEEDS_Y), w2s_ref[...], w2n_ref[...], w3_ref[...])
    ones = jnp.ones((SEEDS_Y, H), BF16)
    grad_rows = inner_rows(belongs, grad_two).astype(BF16)
    scale_rows = inner_rows(belongs, (ones * scale).astype(BF16))
    grad_mean = outer_cols(grad_rows, w2n_ref[...]) / scale_rows
    grad = jnp.where(inner_rows(kept, ones) > 0.5, grad_mean, 0.0)
    grad = jnp.where(inner_rows(is_head, ones) > 0.5, outer_cols(grad_rows, w2s_ref[...]), grad)
    grad_one = inner_rows(left_ref[...], (grad * slope_one).astype(BF16))
    for y in range(Y):
        stage[pl.ds(y * BACK, 32), :] = grad_one[y * 32 :][:32]
        stage[pl.ds(y * BACK + 32, SEEDS_Y), :] = head.astype(F32)
        stage[pl.ds(y * BACK + 32 + SEEDS_Y, SEEDS_Y), :] = mean_two.astype(F32)
    o_ref[...] = stage[...].astype(BF16)


def seeds(pre_one, left, counts, labels, w2_self, w2_nbr, w3):
    return pl.pallas_call(
        seeds_kernel,
        out_shape=jax.ShapeDtypeStruct((Y * BACK, H), BF16),
        in_specs=[VMEM] * 7,
        out_specs=VMEM,
        scratch_shapes=[pltpu.VMEM((Y * BACK, H), F32)],
        compiler_params=pltpu.CompilerParams(vmem_limit_bytes=32 * 1024 * 1024),
        name="seeds",
    )(pre_one, left, counts, labels, w2_self, w2_nbr, w3)


def weights_kernel(r_ref, labels_ref, w2s_ref, w2n_ref, w3_ref, keep_ref, send_ref, o_ref):
    rows = r_ref[...].astype(F32)
    grad_one = jnp.zeros((32, H), F32)
    head, mean_two = [], []
    for y in range(Y):
        grad_one = grad_one + rows[y * BACK :][:32]
        head.append(rows[y * BACK + 32 :][:SEEDS_Y])
        mean_two.append(rows[y * BACK + 32 + SEEDS_Y :][:SEEDS_Y])
    head = jnp.concatenate(head, 0).astype(BF16)
    mean_two = jnp.concatenate(mean_two, 0).astype(BF16)
    act_two, grad_three, grad_two = top(head, mean_two, as_column(labels_ref, 0, SEEDS_B), w2s_ref[...], w2n_ref[...], w3_ref[...])
    o_ref[pl.ds(0, H), :] = inner_rows(head, grad_two)
    o_ref[pl.ds(H, H), :] = inner_rows(mean_two, grad_two)
    o_ref[pl.ds(AT_FIRST, 32), :] = grad_one
    o_ref[pl.ds(AT_THIRD, C), :] = inner_rows(grad_three, act_two)
    rest = 2 * HALF - AT_THIRD - C
    o_ref[pl.ds(AT_THIRD + C, rest), :] = jnp.zeros((rest, H), F32)
    core = lax.axis_index("core")
    keep_ref[...] = o_ref[pl.ds(pl.multiple_of(core * HALF, 8), HALF), :]
    send_ref[...] = o_ref[pl.ds(pl.multiple_of((1 - core) * HALF, 8), HALF), :]


def weights(received, labels, w2_self, w2_nbr, w3):
    return pl.pallas_call(
        weights_kernel,
        out_shape=(jax.ShapeDtypeStruct((HALF, H), F32), jax.ShapeDtypeStruct((HALF, H), F32)),
        in_specs=[VMEM] * 5,
        out_specs=(VMEM, VMEM),
        scratch_shapes=[pltpu.VMEM((2 * HALF, H), F32)],
        compiler_params=pltpu.CompilerParams(vmem_limit_bytes=32 * 1024 * 1024),
        name="weights",
    )(received, labels, w2_self, w2_nbr, w3)


def halve_kernel(kept_ref, other_ref, o_ref):
    total = (kept_ref[...] + other_ref[...]).astype(BF16)
    for x in range(X):
        o_ref[pl.ds(x * HALF, HALF), :] = total


def halve(kept, other):
    return pl.pallas_call(
        halve_kernel,
        out_shape=jax.ShapeDtypeStruct((X * HALF, H), BF16),
        in_specs=[VMEM, VMEM],
        out_specs=VMEM,
        compiler_params=pltpu.CompilerParams(vmem_limit_bytes=16 * 1024 * 1024),
        name="halve",
    )(kept, other)


def finish_kernel(g_ref, w1s_ref, w1n_ref, w2s_ref, w2n_ref, w3_ref, sems):
    copies = [
        pltpu.make_async_copy(g_ref.at[pl.ds(0, H), :], w2s_ref, sems.at[0]),
        pltpu.make_async_copy(g_ref.at[pl.ds(H, H), :], w2n_ref, sems.at[1]),
    ]
    for copy in copies:
        copy.start()
    first = g_ref[pl.ds(AT_FIRST, 32), :]
    w1s_ref[...] = first[:COLS]
    w1n_ref[...] = first[16 : 16 + COLS]
    w3_ref[...] = g_ref[pl.ds(AT_THIRD, C), :]
    for copy in copies:
        copy.wait()


def finish(gradients):
    shapes = [(COLS, H), (COLS, H), (H, H), (H, H), (C, H)]
    anywhere = pl.BlockSpec(memory_space=pl.ANY)
    return pl.pallas_call(
        finish_kernel,
        out_shape=tuple(jax.ShapeDtypeStruct(shape, F32) for shape in shapes),
        in_specs=[VMEM],
        out_specs=(VMEM, VMEM, anywhere, anywhere, VMEM),
        scratch_shapes=[pltpu.SemaphoreType.DMA((2,))],
        compiler_params=pltpu.CompilerParams(vmem_limit_bytes=16 * 1024 * 1024),
        name="finish",
    )(gradients)


def exchange(rows, axis, parts):
    received = lax.all_to_all(rows.reshape(parts, -1, rows.shape[1]), axis, 0, 0)
    return received.reshape(rows.shape)


def local(features, nbr_ids, nbr_counts, self_ids, seed_counts, labels, w1_self, w1_nbr, w2_self, w2_nbr, w3):
    packed = gather(self_ids, nbr_ids.T, nbr_counts, features, w1_self, w1_nbr)
    shares, left = project(exchange(packed, "y", Y))
    pre_one = exchange(spread(exchange(shares, "z", Z)), "z", Z)
    back = seeds(pre_one, left, seed_counts, labels, w2_self, w2_nbr, w3.T)
    kept, sent = weights(exchange(back, "y", Y), labels, w2_self, w2_nbr, w3.T)
    grads = exchange(halve(kept, lax.ppermute(sent, "core", [(0, 1), (1, 0)])), "x", X)
    summed = jnp.sum(grads.reshape(X, HALF, H).astype(F32), axis=0)
    whole = lax.all_gather(summed, "core", axis=0, tiled=True)
    grad_w1s, grad_w1n, grad_w2s, grad_w2n, grad_w3 = finish(whole)
    return grad_w1s, grad_w1n, grad_w2s, grad_w2n, grad_w3.T


def solution(mesh):
    split = Mesh(mesh.devices.reshape(Z, Y, X, CORE), ("z", "y", "x", "core"))
    feat, batch = P(("z", "y"), None), P(("x", "core"))
    in_specs = (feat, P(("x", "core"), None), batch, batch, batch, batch, feat, feat, P(), P(), P())
    out_specs = (feat, feat, P(), P(), P())
    return jax.shard_map(local, mesh=split, in_specs=in_specs, out_specs=out_specs, check_vma=False)
```

```python
import jax
import jax.numpy as jnp
from jax import lax
from jax.experimental import pallas as pl
from jax.experimental.pallas import tpu as pltpu
from jax.sharding import Mesh, PartitionSpec as P

NODES = 65536
COLS = 11
H = 256
C = 172
FAN1 = 15
FAN2 = 10
IDS = 1 + FAN1
KEEP = 1 + FAN2
SEEDS_B = 192
ROWS_B = SEEDS_B * KEEP
Z, Y, X, CORE = 12, 8, 4, 2
BATCH = X * CORE
LOSS_SCALE = 1.0 / (SEEDS_B * BATCH)
SEEDS_Y = SEEDS_B // Y
ROWS_Y = SEEDS_Y * KEEP
GROUPS = 3
PACKED = ROWS_Y // GROUPS
SLOTS = 8
SLOT_ROWS = NODES // SLOTS
CHUNK = 64
CHUNKS = ROWS_B // CHUNK
AHEAD = 4
WIDE = 24
SEND = 144
SHARE = 24
ROWS_Z = Z * SHARE
BACK = WIDE + 2 * SEEDS_Y
AT_FIRST = 2 * H
AT_THIRD = AT_FIRST + WIDE
HALF = 368
PIECES = 2
BF16 = jnp.bfloat16
F32 = jnp.float32
VMEM = pl.BlockSpec(memory_space=pltpu.VMEM)
HBM = pl.BlockSpec(memory_space=pltpu.HBM)


def gather_kernel(
    self_in, nbr_in, counts_in, x_in, w1s_in, w1n_in, o_ref,
    self_ref, nbr_ref, counts_ref, x_ref, w1s_ref, w1n_ref, small_sems, x_sems,
    table, own_ref, agg_ref, ids, near, sems,
):
    lane = lax.broadcasted_iota(jnp.int32, (1, 128), 1)
    small = [(self_in, self_ref), (nbr_in, nbr_ref), (counts_in, counts_ref), (w1s_in, w1s_ref), (w1n_in, w1n_ref)]
    small = [pltpu.make_async_copy(source, target, small_sems.at[i]) for i, (source, target) in enumerate(small)]
    for copy in small:
        copy.start()
    pieces = []
    for piece in range(PIECES):
        pieces.append([])
        for slot in range(SLOTS):
            place = pl.ds(slot * SLOT_ROWS + piece * (SLOT_ROWS // PIECES), SLOT_ROWS // PIECES)
            pieces[piece].append(pltpu.make_async_copy(x_in.at[:, place], x_ref.at[:, place], x_sems.at[piece, slot]))
            pieces[piece][slot].start()
    def fetch(chunk, slot):
        return pltpu.make_async_copy(ids.at[chunk], near[slot], sems.at[slot])

    def tabulate(piece):
        for copy in pieces[piece]:
            copy.wait()

        @pl.loop(0, SLOT_ROWS // PIECES // 128, unroll=8)
        def _(step):
            block = step + piece * (SLOT_ROWS // PIECES // 128)
            stacked = []
            for slot in range(SLOTS):
                start = pl.multiple_of(slot * SLOT_ROWS + block * 128, 128)
                stacked += [x_ref[:, pl.ds(start, 128)].astype(F32), jnp.ones((1, 128), F32), jnp.zeros((4, 128), F32)]
            turned = jnp.concatenate(stacked, 0).astype(BF16).T.astype(F32)
            for slot in range(SLOTS):
                start = pl.multiple_of(slot * SLOT_ROWS + block * 128, 128)
                table[pl.ds(start, 128), :] = jnp.where(lane // 16 == slot, turned, 0.0)

    tabulate(0)
    for copy in small:
        copy.wait()
    counts = counts_ref[...][None, :]
    valid = lax.broadcasted_iota(jnp.int32, (FAN1, ROWS_B), 0) < counts
    both = jnp.concatenate([jnp.where(valid, nbr_ref[...], NODES), self_ref[...][None, :]], 0)
    both = jnp.concatenate([both, jnp.zeros((IDS, CHUNK), jnp.int32)], 1)
    for tile in range(-(-ROWS_B // 128)):
        low, high = both[:8, tile * 128 :][:, :128], both[8:, tile * 128 :][:, :128]
        ids[2 * tile] = jnp.where(lane < CHUNK, low, pltpu.roll(high, CHUNK, 1))
        if 2 * tile + 1 < CHUNKS:
            ids[2 * tile + 1] = jnp.where(lane < CHUNK, pltpu.roll(low, CHUNK, 1), high)
    for slot in range(AHEAD):
        fetch(slot, slot).start()
    for piece in range(1, PIECES):
        tabulate(piece)
    table[pl.ds(NODES, 8), :] = jnp.zeros((8, 128), F32)

    def take(chunk, slot):
        fetch(chunk, slot).wait()
        first = chunk * CHUNK
        for i in range(CHUNK):
            rows = [table[pl.ds(near[slot][j % 8, j // 8 * CHUNK + i], 1), :] for j in range(IDS)]
            own_ref[pl.ds(first + i, 1), :] = rows.pop()
            while len(rows) > 1:
                rows = [sum(rows[a : a + 2]) for a in range(0, len(rows), 2)]
            agg_ref[pl.ds(first + i, 1), :] = rows[0]

    @pl.loop(0, CHUNKS // AHEAD)
    def _(turn):
        for slot in range(AHEAD):
            chunk = turn * AHEAD + slot
            take(chunk, slot)

            @pl.when(chunk + AHEAD < CHUNKS)
            def _():
                fetch(chunk + AHEAD, slot).start()

    for slot in range(CHUNKS % AHEAD):
        take(CHUNKS // AHEAD * AHEAD + slot, slot)

    def halves(low, high, width):
        mask = lane % (2 * width) < width
        if high is None:
            return jnp.where(mask, low + pltpu.roll(low, 128 - width, 1), 0.0)
        moved = jnp.where(mask, pltpu.roll(low, 128 - width, 1), pltpu.roll(high, width, 1))
        return jnp.where(mask, low, high) + moved

    w1 = jnp.concatenate([w1s_ref[...].astype(F32), w1n_ref[...].astype(F32), jnp.zeros((WIDE - 2 * COLS, H), F32)], 0)
    w1 = [w1[:, :128], w1[:, 128:], jnp.zeros((SEND - PACKED - 2 * WIDE, 128), F32)]
    row = lax.broadcasted_iota(jnp.int32, (128, 128), 0)
    column = lax.broadcasted_iota(jnp.int32, (128, 128), 1)
    counter = jnp.where((row % 16 == COLS) & (row // 16 == column // 16), 1.0, 0.0).astype(BF16)

    @pl.loop(0, Y, unroll=2)
    def _(block):
        message = []
        for step in range(PACKED // 8):
            v = []
            for group in range(GROUPS):
                place = pl.ds(pl.multiple_of(block * ROWS_Y + group * PACKED + step * 8, 8), 8)
                v += [own_ref[place, :], agg_ref[place, :]]
            v = [halves(v[q], v[q + 4] if q < 2 else None, 64) for q in range(4)]
            v = [halves(v[q], v[q + 2], 32) for q in range(2)]
            message.append(halves(v[0], v[1], 16))
        packed = jnp.concatenate(message, 0)
        counted = jnp.dot(packed.astype(BF16), counter, preferred_element_type=F32)
        packed = jnp.where((lane < GROUPS * 32) & (lane % 16 < COLS), packed / counted, 0.0)
        message = jnp.concatenate([packed] + w1, 0).astype(BF16)
        o_ref[pl.ds(pl.multiple_of(block * SEND, 16), SEND), :] = message


def gather(self_ids, nbr_ids, counts, features, w1_self, w1_nbr):
    return pl.pallas_call(
        gather_kernel,
        out_shape=jax.ShapeDtypeStruct((Y * SEND, 128), BF16),
        in_specs=[HBM] * 6,
        out_specs=VMEM,
        scratch_shapes=[
            pltpu.VMEM((ROWS_B,), jnp.int32),
            pltpu.VMEM((FAN1, ROWS_B), jnp.int32),
            pltpu.VMEM((ROWS_B,), jnp.int32),
            pltpu.VMEM((COLS, NODES), BF16),
            pltpu.VMEM((COLS, H), BF16),
            pltpu.VMEM((COLS, H), BF16),
            pltpu.SemaphoreType.DMA((5,)),
            pltpu.SemaphoreType.DMA((PIECES, SLOTS)),
            pltpu.VMEM((NODES + 8, 128), F32),
            pltpu.VMEM((ROWS_B, 128), F32),
            pltpu.VMEM((ROWS_B, 128), F32),
            pltpu.VMEM((CHUNKS, 8, 128), jnp.int32),
            [pltpu.SMEM((8, 128), jnp.int32)] * AHEAD,
            pltpu.SemaphoreType.DMA((AHEAD,)),
        ],
        compiler_params=pltpu.CompilerParams(vmem_limit_bytes=63 * 1024 * 1024),
        name="gather",
    )(self_ids, nbr_ids, counts, features, w1_self, w1_nbr)


def project_kernel(r_ref, o_ref, left_ref):
    lane = lax.broadcasted_iota(jnp.int32, (1, 128), 1)
    blocks = [r_ref[pl.ds(y * SEND, SEND), :].astype(F32) for y in range(Y)]
    right = []
    gap = jnp.zeros((16 - COLS, H), F32)
    for block in blocks:
        rows = jnp.concatenate([block[PACKED + half * WIDE :][:WIDE] for half in range(2)], 1)
        right += [rows[:COLS], gap, rows[COLS : 2 * COLS], gap]
    right = jnp.concatenate(right, 0).astype(BF16)
    left = []
    for group in range(GROUPS):
        halves = []
        for half in range(2):
            mixed = jnp.zeros((PACKED, 128), F32)
            for j in range(4):
                one = blocks[half * 4 + j][:PACKED]
                shift = (j - group) * 32 % 128
                one = pltpu.roll(one, shift, 1) if shift else one
                mixed = jnp.where(lane // 32 == j, one, mixed)
            halves.append(mixed)
        left.append(jnp.concatenate(halves, 1))
    left = jnp.concatenate(left, 0).astype(BF16)
    left_ref[...] = left
    total = jnp.dot(left, right, preferred_element_type=F32)
    o_ref[...] = jnp.concatenate([total, jnp.zeros((ROWS_Z - ROWS_Y, H), F32)], 0).astype(BF16)


def project(received):
    return pl.pallas_call(
        project_kernel,
        out_shape=(jax.ShapeDtypeStruct((ROWS_Z, H), BF16), jax.ShapeDtypeStruct((ROWS_Y, Y * 32), BF16)),
        in_specs=[VMEM],
        out_specs=(VMEM, VMEM),
        compiler_params=pltpu.CompilerParams(vmem_limit_bytes=32 * 1024 * 1024),
        name="project",
    )(received)


def spread_kernel(s_ref, o_ref):
    total = jnp.zeros((SHARE, H), F32)
    for pair in range(Z // 2):
        both = s_ref[pl.ds(pair * 2 * SHARE, 2 * SHARE), :].astype(F32)
        total = total + (both[:SHARE] + both[SHARE:])
    twice = jnp.concatenate([total, total], 0).astype(BF16)
    for pair in range(Z // 2):
        o_ref[pl.ds(pair * 2 * SHARE, 2 * SHARE), :] = twice


def spread(shares):
    return pl.pallas_call(
        spread_kernel,
        out_shape=jax.ShapeDtypeStruct((ROWS_Z, H), BF16),
        in_specs=[VMEM],
        out_specs=VMEM,
        compiler_params=pltpu.CompilerParams(vmem_limit_bytes=16 * 1024 * 1024),
        name="spread",
    )(shares)


def sigmoid(value):
    return 1.0 / (1.0 + jnp.exp(-value))


def outer_cols(left, right):
    return lax.dot_general(left, right, (((1,), (1,)), ((), ())), preferred_element_type=F32)


def inner_rows(left, right):
    return lax.dot_general(left, right, (((0,), (0,)), ((), ())), preferred_element_type=F32)


def top(head, mean_two, labels, w2_self, w2_nbr, w3):
    pre_two = jnp.dot(head, w2_self, preferred_element_type=F32) + jnp.dot(mean_two, w2_nbr, preferred_element_type=F32)
    sig_two = sigmoid(pre_two)
    act_two = (pre_two * sig_two).astype(BF16)
    slope_two = sig_two * (1.0 + pre_two * (1.0 - sig_two))
    logits = outer_cols(act_two, w3)
    expsum = jnp.exp(logits - jnp.max(logits, axis=1, keepdims=True))
    probability = expsum / jnp.sum(expsum, axis=1, keepdims=True)
    onehot = (lax.broadcasted_iota(jnp.int32, logits.shape, 1) == labels).astype(F32)
    grad_three = ((probability - onehot) * LOSS_SCALE).astype(BF16)
    grad_two = (jnp.dot(grad_three, w3, preferred_element_type=F32) * slope_two).astype(BF16)
    return act_two, grad_three, grad_two


def as_column(ref, first, rows):
    row = lax.broadcasted_iota(jnp.int32, (rows, SEEDS_B), 0) + first
    column = lax.broadcasted_iota(jnp.int32, (rows, SEEDS_B), 1)
    spread_out = jnp.where(row == column, ref[...][None, :], 0).astype(F32)
    return jnp.sum(spread_out, axis=1, keepdims=True).astype(jnp.int32)


def seeds_kernel(z_ref, left_ref, counts_ref, labels_ref, w2s_ref, w2n_ref, w3_ref, o_ref, stage):
    first = lax.axis_index("y") * SEEDS_Y
    counts = as_column(counts_ref, first, SEEDS_Y)
    scale = counts.astype(F32)
    pre_one = z_ref[...].astype(F32)[:ROWS_Y]
    sig_one = sigmoid(pre_one)
    act_one = (pre_one * sig_one).astype(BF16)
    slope_one = sig_one * (1.0 + pre_one * (1.0 - sig_one))
    behind = lax.broadcasted_iota(jnp.int32, (SEEDS_Y, ROWS_Y), 1) - KEEP * lax.broadcasted_iota(jnp.int32, (SEEDS_Y, ROWS_Y), 0)

    def choose(mask):
        return jnp.where(mask, 1.0, 0.0).astype(BF16)

    kept = choose((behind > 0) & (behind <= counts))
    belongs = choose((behind >= 0) & (behind < KEEP))
    is_head = choose(behind == 0)
    head = jnp.dot(is_head, act_one, preferred_element_type=F32).astype(BF16)
    mean_two = (jnp.dot(kept, act_one, preferred_element_type=F32) / scale).astype(BF16)
    _, _, grad_two = top(head, mean_two, as_column(labels_ref, first, SEEDS_Y), w2s_ref[...], w2n_ref[...], w3_ref[...])
    ones = jnp.ones((SEEDS_Y, H), BF16)
    grad_rows = inner_rows(belongs, grad_two).astype(BF16)
    scale_rows = inner_rows(belongs, (ones * scale).astype(BF16))
    grad_mean = outer_cols(grad_rows, w2n_ref[...]) / scale_rows
    grad = jnp.where(inner_rows(kept, ones) > 0.5, grad_mean, 0.0)
    grad = jnp.where(inner_rows(is_head, ones) > 0.5, outer_cols(grad_rows, w2s_ref[...]), grad)
    grad_one = inner_rows(left_ref[...], (grad * slope_one).astype(BF16))
    for y in range(Y):
        both = grad_one[y * 32 :][:32]
        none = jnp.zeros((WIDE - 2 * COLS, H), F32)
        stage[pl.ds(y * BACK, WIDE), :] = jnp.concatenate([both[:COLS], both[16 : 16 + COLS], none], 0)
        stage[pl.ds(y * BACK + WIDE, SEEDS_Y), :] = head.astype(F32)
        stage[pl.ds(y * BACK + WIDE + SEEDS_Y, SEEDS_Y), :] = mean_two.astype(F32)
    o_ref[...] = stage[...].astype(BF16)


def seeds(pre_one, left, counts, labels, w2_self, w2_nbr, w3):
    return pl.pallas_call(
        seeds_kernel,
        out_shape=jax.ShapeDtypeStruct((Y * BACK, H), BF16),
        in_specs=[VMEM] * 7,
        out_specs=VMEM,
        scratch_shapes=[pltpu.VMEM((Y * BACK, H), F32)],
        compiler_params=pltpu.CompilerParams(vmem_limit_bytes=32 * 1024 * 1024),
        name="seeds",
    )(pre_one, left, counts, labels, w2_self, w2_nbr, w3)


def weights_kernel(r_ref, labels_ref, w2s_ref, w2n_ref, w3_ref, keep_ref, send_ref, o_ref):
    rows = r_ref[...].astype(F32)
    grad_one = jnp.zeros((WIDE, H), F32)
    head, mean_two = [], []
    for y in range(Y):
        grad_one = grad_one + rows[y * BACK :][:WIDE]
        head.append(rows[y * BACK + WIDE :][:SEEDS_Y])
        mean_two.append(rows[y * BACK + WIDE + SEEDS_Y :][:SEEDS_Y])
    head = jnp.concatenate(head, 0).astype(BF16)
    mean_two = jnp.concatenate(mean_two, 0).astype(BF16)
    act_two, grad_three, grad_two = top(head, mean_two, as_column(labels_ref, 0, SEEDS_B), w2s_ref[...], w2n_ref[...], w3_ref[...])
    o_ref[pl.ds(0, H), :] = inner_rows(head, grad_two)
    o_ref[pl.ds(H, H), :] = inner_rows(mean_two, grad_two)
    o_ref[pl.ds(AT_FIRST, WIDE), :] = grad_one
    o_ref[pl.ds(AT_THIRD, C), :] = inner_rows(grad_three, act_two)
    rest = 2 * HALF - AT_THIRD - C
    o_ref[pl.ds(AT_THIRD + C, rest), :] = jnp.zeros((rest, H), F32)
    core = lax.axis_index("core")
    keep_ref[...] = o_ref[pl.ds(pl.multiple_of(core * HALF, 8), HALF), :]
    send_ref[...] = o_ref[pl.ds(pl.multiple_of((1 - core) * HALF, 8), HALF), :]


def weights(received, labels, w2_self, w2_nbr, w3):
    return pl.pallas_call(
        weights_kernel,
        out_shape=(jax.ShapeDtypeStruct((HALF, H), F32), jax.ShapeDtypeStruct((HALF, H), F32)),
        in_specs=[VMEM] * 5,
        out_specs=(VMEM, VMEM),
        scratch_shapes=[pltpu.VMEM((2 * HALF, H), F32)],
        compiler_params=pltpu.CompilerParams(vmem_limit_bytes=32 * 1024 * 1024),
        name="weights",
    )(received, labels, w2_self, w2_nbr, w3)


def halve_kernel(kept_ref, other_ref, o_ref):
    total = (kept_ref[...] + other_ref[...]).astype(BF16)
    for x in range(X):
        o_ref[pl.ds(x * HALF, HALF), :] = total


def halve(kept, other):
    return pl.pallas_call(
        halve_kernel,
        out_shape=jax.ShapeDtypeStruct((X * HALF, H), BF16),
        in_specs=[VMEM, VMEM],
        out_specs=VMEM,
        compiler_params=pltpu.CompilerParams(vmem_limit_bytes=16 * 1024 * 1024),
        name="halve",
    )(kept, other)


def finish_kernel(g_ref, w1s_ref, w1n_ref, w2s_ref, w2n_ref, w3_ref, sems):
    copies = [
        pltpu.make_async_copy(g_ref.at[pl.ds(0, H), :], w2s_ref, sems.at[0]),
        pltpu.make_async_copy(g_ref.at[pl.ds(H, H), :], w2n_ref, sems.at[1]),
    ]
    for copy in copies:
        copy.start()
    first = g_ref[pl.ds(AT_FIRST, WIDE), :]
    w1s_ref[...] = first[:COLS]
    w1n_ref[...] = first[COLS : 2 * COLS]
    w3_ref[...] = g_ref[pl.ds(AT_THIRD, C), :]
    for copy in copies:
        copy.wait()


def finish(gradients):
    shapes = [(COLS, H), (COLS, H), (H, H), (H, H), (C, H)]
    anywhere = pl.BlockSpec(memory_space=pl.ANY)
    return pl.pallas_call(
        finish_kernel,
        out_shape=tuple(jax.ShapeDtypeStruct(shape, F32) for shape in shapes),
        in_specs=[VMEM],
        out_specs=(VMEM, VMEM, anywhere, anywhere, VMEM),
        scratch_shapes=[pltpu.SemaphoreType.DMA((2,))],
        compiler_params=pltpu.CompilerParams(vmem_limit_bytes=16 * 1024 * 1024),
        name="finish",
    )(gradients)


def exchange(rows, axis, parts):
    received = lax.all_to_all(rows.reshape(parts, -1, rows.shape[1]), axis, 0, 0)
    return received.reshape(rows.shape)


def local(features, nbr_ids, nbr_counts, self_ids, seed_counts, labels, w1_self, w1_nbr, w2_self, w2_nbr, w3):
    packed = gather(self_ids, nbr_ids.T, nbr_counts, features, w1_self, w1_nbr)
    shares, left = project(exchange(packed, "y", Y))
    pre_one = exchange(spread(exchange(shares, "z", Z)), "z", Z)
    back = seeds(pre_one, left, seed_counts, labels, w2_self, w2_nbr, w3.T)
    kept, sent = weights(exchange(back, "y", Y), labels, w2_self, w2_nbr, w3.T)
    grads = exchange(halve(kept, lax.ppermute(sent, "core", [(0, 1), (1, 0)])), "x", X)
    summed = jnp.sum(grads.reshape(X, HALF, H).astype(F32), axis=0)
    whole = lax.all_gather(summed, "core", axis=0, tiled=True)
    grad_w1s, grad_w1n, grad_w2s, grad_w2n, grad_w3 = finish(whole)
    return grad_w1s, grad_w1n, grad_w2s, grad_w2n, grad_w3.T


def solution(mesh):
    split = Mesh(mesh.devices.reshape(Z, Y, X, CORE), ("z", "y", "x", "core"))
    feat, batch = P(("z", "y"), None), P(("x", "core"))
    in_specs = (feat, P(("x", "core"), None), batch, batch, batch, batch, feat, feat, P(), P(), P())
    out_specs = (feat, feat, P(), P(), P())
    return jax.shard_map(local, mesh=split, in_specs=in_specs, out_specs=out_specs, check_vma=False)
```
